32 devices in a mesh: sec: 16 (over z, y, core), op: 2 (over x).
Axes of the slice: x: 2, y: 2, z: 4, core: 2. Of those that a mesh axis runs over, the one named last changes fastest.
Arguments:
- wave: bfloat16 [96, 256, 256], P('sec', 'op'), may hold values from -6 to 6
- left_ops: bfloat16 [96, 16, 256, 256], P('sec', 'op'), may hold values from -0.125 to 0.125
- right_ops: bfloat16 [96, 16, 256, 256], P('sec', 'op'), may hold values from -0.375 to 0.375
- owner_map: int32 [96, 5], P('sec'), may hold values from 0 to 15, all different within a row; in each aligned block of 6 rows (0 to 5, 6 to 11, ...) at most 3 rows name the same one
- local_map: int32 [96, 5], P('sec'), may hold values from 0 to 5
- op_class: int32 [16], P('op'), may hold values from 0 to 4
Outputs:
- applied: bfloat16 [96, 256, 256], P('sec', 'op')
The draws below stay inside these ranges and needn't reach their ends.
Inputs may be any that keep to these rules, and one draw needn't show every extreme that they name: `owner_map`: each row names 5 different owners; among the rows of one sec index no owner is named more than 3 times, and that count is reached.
All inputs are finite; a program needn't handle non-finite values.
Results may differ from the reference program's by a relative error of at most 0.0049.
Values may be sent and summed in bfloat16 or wider, within the bound.
No kernel may reach another device: no remote copies, remote signals or barrier semaphores. Data moves between devices by JAX's collectives and lax.ppermute only.
A program may use at most 128 MiB of HBM per device.

```python
import math
import jax
import jax.numpy as jnp
import numpy as np
from jax import lax

B = 256
NCLS = 5
SEC_DEV = 6
NOPS = 16
SECTORS = 96
CAP = 3
N_SEC = 16


def draw_op_class(key, part):
    order = jax.random.permutation(jax.random.fold_in(key, 11), NOPS).astype(jnp.int32)
    offset = jax.random.randint(jax.random.fold_in(key, 13), (), 0, NCLS).astype(jnp.int32)
    return ((order + offset) % NCLS).astype(jnp.int32)


def place_ends(result, own_key, smallest, top_value):
    place = [jax.random.randint(jax.random.fold_in(own_key, axis), (), 0, length) for axis, length in enumerate(result.shape)]
    main_axis = result.shape.index(max(result.shape))
    neighbour = place[:main_axis] + [(place[main_axis] + 1) % result.shape[main_axis]] + place[main_axis + 1:]
    return result.at[tuple(place)].set(smallest).at[tuple(neighbour)].set(top_value)


def spiked(drawn, stream_key, source, target, parts, factor):
    owner, partner = [(jnp.arange(drawn.shape[dim]) // (drawn.shape[dim] // parts)).reshape([-1 if axis == dim else 1 for axis in range(drawn.ndim)]) for dim in (source, target)]
    chosen = jax.random.permutation(stream_key, parts)[partner]
    strong = (owner == chosen) | (owner == (partner + parts // 2) % parts)
    return jnp.where(strong, factor * drawn, drawn)


def level_of(stream_key, dims, pieces, least, largest):
    level = 1.0
    for dim, shards_of in pieces:
        heights = jax.random.uniform(jax.random.fold_in(jax.random.fold_in(stream_key, 6), dim), (shards_of,), jnp.float32, least / len(pieces), largest / len(pieces))
        level = level * jnp.repeat(jnp.exp(heights), dims[dim] // shards_of).reshape((-1,) + (1,) * (len(dims) - 1 - dim))
    return level


def shared_out(rng, own, number, rows, count, top, limit, slope):
    sequence = jax.random.permutation(rng, count)
    packed, ordinary = load_shares(count, rows * top, limit, slope, True), load_shares(count, rows * top, limit, slope, False)
    places = jnp.arange(count)

    def named(sizes, turn):
        used = int((sizes > 0).sum())
        fixed = max(1, used // 4)
        passed = fixed + (places - fixed + turn * (used - fixed)) % max(1, count - fixed)
        return jnp.zeros((count,), jnp.int32).at[sequence[jnp.where(places < fixed, places, passed)]].set(jnp.asarray(sizes, jnp.int32))

    sizes = jnp.where(number % 4 == 0, named(packed, number // 4), named(ordinary, number - number // 4 - 1))
    mixed = jax.random.permutation(jax.random.fold_in(own, 3), count)
    source_of, sink = mixed[0:count // 2 * 2:2], mixed[1:count // 2 * 2:2]
    slack = jnp.minimum(sizes[source_of] - 1, limit - sizes[sink]) // 2
    slack = jnp.where((source_of == sequence[0]) | (sink == sequence[0]) | (sizes[sink] == 0), 0, jnp.maximum(slack, 0))
    passed = jax.random.randint(jax.random.fold_in(own, 4), (count // 2,), 0, 1 << 20) % (slack + 1)
    sizes = sizes.at[source_of].add(-passed).at[sink].add(passed)
    items = jnp.searchsorted(jnp.cumsum(sizes), jnp.arange(rows * top), side="right").astype(jnp.int32)
    table = items.reshape(top, rows).T
    table = table[jax.random.permutation(jax.random.fold_in(own, 1), rows)]
    turn = jax.random.randint(jax.random.fold_in(own, 2), (rows, 1), 0, top)
    return jnp.take_along_axis(table, (jnp.arange(top)[None, :] + turn) % top, axis=1)


def load_shares(number_of, total, bound, skew, full):
    weights = [(1 << 20) // math.isqrt(standing ** skew) + 1 for standing in range(1, number_of + 1)]
    largest = bound if full else min(bound, max(-(-total // number_of), total * weights[0] // sum(weights)))
    least = 1 if total - largest >= number_of - 1 else 0
    counts, rest = [largest] + [least] * (number_of - 1), total - largest - least * (number_of - 1)
    while rest > 0:
        candidates = [i for i in range(1, number_of) if counts[i] < largest] or [i for i in range(1, number_of) if counts[i] < bound]
        pool, left = sum([weights[i] for i in candidates]), rest
        for i in candidates:
            extra = min(bound - counts[i], max(1, left * weights[i] // pool), rest)
            counts[i] = counts[i] + extra
            rest = rest - extra
    return np.array(counts)


def bell_draw(own_key, dims, spread, most, shards=(), kind=jnp.bfloat16):
    result = jax.random.normal(own_key, dims, jnp.float32) * spread
    if len(shards) > 0:
        result = level_of(own_key, dims, shards, -0.22, 0.18) * result
    return jnp.clip(result, min=-most, max=most).astype(kind)


def heavy_noise(rng, shape, spread, limit, shards, heavy, held_as=jnp.bfloat16):
    drawn = spread * jax.random.normal(rng, shape, jnp.float32)
    if shards:
        drawn = drawn * level_of(rng, shape, shards, -0.22, 0.18)
    return jnp.clip(spiked(drawn, jax.random.fold_in(rng, 3), *heavy), -limit, limit).astype(held_as)


def setup_inputs(seed: int = 0) -> dict:
    splits = jax.random.split(jax.random.key(seed), 7)
    wave = bell_draw(splits[0], (SECTORS, B, B), 1.0, 6.0, ((0, 16), (1, 2)))
    left_ops = heavy_noise(splits[1], (SECTORS, NOPS, B, B), (B * NOPS) ** -0.5, 0.125, ((0, 16), (1, 2)), (1, 2, 2, 2.0))
    right_ops = bell_draw(splits[2], (SECTORS, NOPS, B, B), B ** -0.5, 0.375, ((0, 16), (1, 2)))
    owner_map_keys = jax.random.split(jax.random.fold_in(splits[3], 1), SECTORS // SEC_DEV)
    owner_map_turns = jax.random.permutation(jax.random.fold_in(splits[3], 3), SECTORS // SEC_DEV)
    owner_map = jax.vmap(lambda own, number: shared_out(jax.random.fold_in(splits[3], 2), own, number, SEC_DEV, N_SEC, NCLS, CAP, 2))(owner_map_keys, owner_map_turns).reshape((SECTORS, NCLS))
    local_map = place_ends(jax.random.randint(splits[4], (SECTORS, NCLS), 0, SEC_DEV), jax.random.fold_in(splits[4], 1), 0, SEC_DEV - 1).astype(jnp.int32)
    op_class = draw_op_class(jax.random.fold_in(splits[6], 71), 0)
    return dict(wave=wave, left_ops=left_ops, right_ops=right_ops, owner_map=owner_map, local_map=local_map, op_class=op_class)


def reference(wave, left_ops, right_ops, owner_map, local_map, op_class):
    source = (owner_map[:, op_class] * SEC_DEV + local_map[:, op_class]).astype(jnp.int32)

    def per_target(target_args):
        left_blocks, right_blocks, picked = target_args
        blocks = wave[picked].astype(jnp.float32)
        lifted = jnp.einsum('onk,okm->onm', left_blocks.astype(jnp.float32), blocks).astype(jnp.bfloat16)
        lifted = lax.optimization_barrier(lifted)
        summed = jnp.einsum('onm,okm->nk', lifted.astype(jnp.float32), right_blocks.astype(jnp.float32))
        return summed.astype(jnp.bfloat16)

    return lax.map(per_target, (left_ops, right_ops, source))
```

```python
import functools

import jax
import jax.numpy as jnp
from jax import lax
from jax.experimental import pallas as pl
from jax.experimental.pallas import tpu as pltpu
from jax.sharding import PartitionSpec as P


def products(terms, op_size, owner, local, op_class, mine, *refs):
    blocks, left, right = refs[:terms], refs[terms], refs[terms + 1]
    keep, send, total = refs[terms + 2 :]
    size = left.shape[-1]
    rows = size // op_size
    for o in range(terms):
        block = blocks[o][...].reshape(size, size)
        lifted = jnp.dot(left[0, o], block, preferred_element_type=jnp.float32).astype(jnp.bfloat16)
        term = lax.dot_general(
            lifted, right[0, o], (((1,), (1,)), ((), ())), preferred_element_type=jnp.float32
        )
        if o == 0:
            total[...] = term
        else:
            total[...] += term
    me = mine[0]
    keep[0] = total[pl.ds(pl.multiple_of(me * rows, rows), rows), :]
    for k in range(1, op_size):
        other = lax.rem(me + k, op_size)
        send[k - 1, 0] = total[pl.ds(pl.multiple_of(other * rows, rows), rows), :].astype(jnp.bfloat16)


def shards(wave, left_ops, right_ops, owner_map, local_map, op_class):
    sec_size, op_size = lax.axis_size("sec"), lax.axis_size("op")
    targets, terms, size, _ = left_ops.shape
    sec_dev, rows, _ = wave.shape
    gathered = lax.all_gather(wave, ("sec", "op")).reshape(sec_size, op_size, sec_dev, rows, size)
    mine = lax.axis_index("op").astype(jnp.int32).reshape(1)

    def block_spec(o):
        def place(t, owner, local, op_class, mine):
            c = op_class[o]
            return owner[t, c], 0, local[t, c], 0, 0

        return pl.BlockSpec((1, op_size, 1, rows, size), place)

    ops_spec = pl.BlockSpec((1, terms, size, size), lambda t, *_: (t, 0, 0, 0))
    keep, send = pl.pallas_call(
        functools.partial(products, terms, op_size),
        grid_spec=pltpu.PrefetchScalarGridSpec(
            num_scalar_prefetch=4,
            grid=(targets,),
            in_specs=[block_spec(o) for o in range(terms)] + [ops_spec, ops_spec],
            out_specs=[
                pl.BlockSpec((1, rows, size), lambda t, *_: (t, 0, 0)),
                pl.BlockSpec((op_size - 1, 1, rows, size), lambda t, *_: (0, t, 0, 0)),
            ],
            scratch_shapes=[pltpu.VMEM((size, size), jnp.float32)],
        ),
        out_shape=[
            jax.ShapeDtypeStruct((targets, rows, size), jnp.float32),
            jax.ShapeDtypeStruct((op_size - 1, targets, rows, size), jnp.bfloat16),
        ],
        compiler_params=pltpu.CompilerParams(vmem_limit_bytes=32 * 1024 * 1024),
        cost_estimate=pl.CostEstimate(
            flops=4 * targets * terms * size**3,
            bytes_accessed=6 * targets * terms * size**2,
            transcendentals=0,
        ),
    )(owner_map, local_map, op_class, mine, *([gathered] * terms), left_ops, right_ops)
    for k in range(1, op_size):
        turn = [(p, (p + k) % op_size) for p in range(op_size)]
        keep = keep + lax.ppermute(send[k - 1], "op", turn).astype(jnp.float32)
    return keep.astype(jnp.bfloat16)


def solution(mesh):
    in_specs = (
        P("sec", "op", None),
        P("sec", "op", None, None),
        P("sec", "op", None, None),
        P("sec", None),
        P("sec", None),
        P("op"),
    )
    out_specs = P("sec", "op", None)
    return jax.shard_map(shards, mesh=mesh, in_specs=in_specs, out_specs=out_specs, check_vma=False)
```

```python
import functools

import jax
import jax.numpy as jnp
from jax import lax
from jax.experimental import pallas as pl
from jax.experimental.pallas import tpu as pltpu
from jax.sharding import PartitionSpec as P


def pack_kernel(places, *refs):
    out, sems = refs[-2], refs[-1]
    copies = []
    for i, (unit, turns, sectors, rows) in enumerate(places):
        target = out.at[unit, pl.ds(*turns), pl.ds(*sectors), pl.ds(*rows)]
        copies.append(pltpu.make_async_copy(refs[i], target, sems.at[i]))
    for copy in copies:
        copy.start()
    for copy in copies:
        copy.wait()


def pack(pieces, shape):
    arrays = [array for array, _ in pieces]
    return pl.pallas_call(
        functools.partial(pack_kernel, [place for _, place in pieces]),
        in_specs=[pl.BlockSpec(memory_space=pl.ANY)] * len(arrays),
        out_specs=pl.BlockSpec(memory_space=pl.ANY),
        out_shape=jax.ShapeDtypeStruct(shape, arrays[0].dtype),
        scratch_shapes=[pltpu.SemaphoreType.DMA((len(arrays),))],
        cost_estimate=pl.CostEstimate(
            flops=0, bytes_accessed=4 * sum(array.size for array in arrays), transcendentals=0
        ),
    )(*arrays)


def products(sizes, table, *refs):
    targets, terms, classes, op_size, batches = sizes
    sources = refs[:batches]
    left, right, keep, send, blocks, total, sems = refs[batches:]
    size = left.shape[-1]
    rows = size // op_size
    asked = targets * classes
    me = table[3 * asked + terms]

    for t in range(targets):

        @pl.loop(0, classes)
        def _(c):
            r = t * classes + c
            where, unit, sector = table[r], table[asked + r], table[2 * asked + r]
            for i, source in enumerate(sources):

                @pl.when(where == i)
                def _():
                    for j in range(op_size):
                        pltpu.make_async_copy(
                            source.at[unit, j, sector],
                            blocks.at[r, lax.rem(me + j, op_size)],
                            sems.at[t],
                        ).start()

    @pl.loop(0, targets)
    def _(t):
        mine = blocks.at[pl.ds(t * classes, classes)]
        pltpu.make_async_copy(mine, mine, sems.at[t]).wait()
        for o in range(terms):
            block = blocks[t * classes + table[3 * asked + o]].reshape(size, size)
            lifted = jnp.dot(left[t, o], block, preferred_element_type=jnp.float32).astype(jnp.bfloat16)
            term = lax.dot_general(
                lifted, right[t, o], (((1,), (1,)), ((), ())), preferred_element_type=jnp.float32
            )
            if o == 0:
                total[...] = term
            else:
                total[...] += term
        keep[t] = total[pl.ds(pl.multiple_of(me * rows, rows), rows), :]
        for k in range(1, op_size):
            other = lax.rem(me + k, op_size)
            send[k - 1, t] = total[pl.ds(pl.multiple_of(other * rows, rows), rows), :].astype(jnp.bfloat16)


def shards(wave, left_ops, right_ops, owner_map, local_map, op_class):
    sec_size, op_size = lax.axis_size("sec"), lax.axis_size("op")
    targets, terms, size, _ = left_ops.shape
    sec_dev, rows, _ = wave.shape
    classes = owner_map.shape[1]
    chips = sec_size // 2
    half = chips // 2
    early = sec_dev // 2
    late = sec_dev - early

    ring = list(range(0, chips, 2)) + list(range(1, chips, 2))[::-1]

    def hop(x, step):
        pairs = [
            (2 * ring[i] + k, 2 * ring[(i + step) % chips] + k) for i in range(chips) for k in range(2)
        ]
        return lax.ppermute(x, "sec", pairs)

    def across(x, j):
        return lax.ppermute(x, "op", [((q + j) % op_size, q) for q in range(op_size)])

    def swap(x):
        return lax.ppermute(x, "sec", [(s, s ^ 1) for s in range(sec_size)])

    first, second = wave[:early], wave[early:]
    crossed = jnp.stack([first] + [across(first, j) for j in range(1, op_size)])

    pieces = [[] for _ in range(chips)]

    def arrived_early(unit, x, turn):
        pieces[unit].append((x, (0, (turn, x.shape[0]), (0, early), (0, rows))))

    def arrived_late(unit, x, row):
        pieces[unit].append((x[None], (0, (0, 1), (early, late), (row, x.shape[1]))))
        for j in range(1, op_size):
            pieces[unit].append((across(x, j)[None], (0, (j, 1), (early, late), (row, x.shape[1]))))

    arrived_early(0, crossed, 0)
    arrived_late(0, second, 0)
    ahead = {-1: (crossed, second), 1: (crossed, second)}
    for d in range(1, half):
        for step in (-1, 1):
            wide, narrow = ahead[step]
            narrow = hop(narrow, step)
            wide = hop(wide, step)
            ahead[step] = wide, narrow
            unit = 2 * d - 1 + (step > 0)
            arrived_late(unit, narrow, 0)
            arrived_early(unit, wide, 0)
    cut, turn = rows // 2, op_size // 2
    arrived_late(chips - 1, hop(ahead[-1][1][:, :cut], -1), 0)
    arrived_late(chips - 1, hop(ahead[1][1][:, cut:], 1), cut)
    arrived_early(chips - 1, hop(ahead[-1][0][:turn], -1), 0)
    arrived_early(chips - 1, hop(ahead[1][0][turn:], 1), turn)

    bounds = [0, chips - 3, chips - 1, chips]
    sources = []
    for low, high in zip(bounds[:-1], bounds[1:]):
        placed = [
            (x, (unit - low,) + place[1:]) for unit in range(low, high) for x, place in pieces[unit]
        ]
        packed = pack(placed, (high - low, op_size, sec_dev, rows, size))
        sources += [packed, swap(packed)]

    me_sec = lax.axis_index("sec").astype(jnp.int32)

    def position(chip):
        return jnp.where(chip % 2 == 0, chip // 2, chips - 1 - chip // 2)

    owner = owner_map.reshape(-1)
    offset = (position(owner // 2) - position(me_sec // 2)) % chips
    distance = jnp.minimum(offset, chips - offset)
    unit = jnp.where(offset == 0, 0, 2 * distance - 1 + (offset > half).astype(jnp.int32))
    batch = sum((unit >= b).astype(jnp.int32) for b in bounds[1:-1])
    start = sum(jnp.where(batch == i, b, 0) for i, b in enumerate(bounds[:-1]))
    table = jnp.concatenate(
        [
            2 * batch + (owner + me_sec) % 2,
            unit - start,
            local_map.reshape(-1),
            op_class,
            lax.axis_index("op").astype(jnp.int32).reshape(1),
        ]
    ).astype(jnp.int32)

    whole = pl.BlockSpec(memory_space=pltpu.VMEM)
    keep, send = pl.pallas_call(
        functools.partial(products, (targets, terms, classes, op_size, len(sources))),
        in_specs=[pl.BlockSpec(memory_space=pltpu.SMEM)]
        + [pl.BlockSpec(memory_space=pl.ANY)] * len(sources)
        + [whole, whole],
        out_specs=[whole, whole],
        out_shape=[
            jax.ShapeDtypeStruct((targets, rows, size), jnp.float32),
            jax.ShapeDtypeStruct((op_size - 1, targets, rows, size), jnp.bfloat16),
        ],
        scratch_shapes=[
            pltpu.VMEM((targets * classes, op_size, rows, size), jnp.bfloat16),
            pltpu.VMEM((size, size), jnp.float32),
            pltpu.SemaphoreType.DMA((targets,)),
        ],
        compiler_params=pltpu.CompilerParams(vmem_limit_bytes=32 * 1024 * 1024),
        cost_estimate=pl.CostEstimate(
            flops=4 * targets * terms * size**3,
            bytes_accessed=6 * targets * terms * size**2,
            transcendentals=0,
        ),
    )(table, *sources, left_ops, right_ops)
    for k in range(1, op_size):
        turn = [(p, (p + k) % op_size) for p in range(op_size)]
        keep = keep + lax.ppermute(send[k - 1], "op", turn).astype(jnp.float32)
    return keep.astype(jnp.bfloat16)


def solution(mesh):
    in_specs = (
        P("sec", "op", None),
        P("sec", "op", None, None),
        P("sec", "op", None, None),
        P("sec", None),
        P("sec", None),
        P("op"),
    )
    out_specs = P("sec", "op", None)
    return jax.shard_map(shards, mesh=mesh, in_specs=in_specs, out_specs=out_specs, check_vma=False)
```

```python
import functools

import jax
import jax.numpy as jnp
from jax import lax
from jax.experimental import pallas as pl
from jax.experimental.pallas import tpu as pltpu
from jax.sharding import Mesh, PartitionSpec as P


def products(sizes, table, *refs):
    targets, terms, classes, op_size, batches = sizes
    sources = refs[:batches]
    left, right, keep, send, blocks, total, sems = refs[batches:]
    size = left.shape[-1]
    rows = size // op_size
    asked = targets * classes
    me = table[3 * asked + terms]

    for t in range(targets):

        @pl.loop(0, classes)
        def _(c):
            r = t * classes + c
            where, unit, sector = table[r], table[asked + r], table[2 * asked + r]
            for i, source in enumerate(sources):

                @pl.when(where == i)
                def _():
                    for j in range(op_size):
                        pltpu.make_async_copy(
                            source.at[unit * op_size + j, sector], blocks.at[r, j], sems.at[t]
                        ).start()

    @pl.loop(0, targets)
    def _(t):
        mine = blocks.at[pl.ds(t * classes, classes)]
        pltpu.make_async_copy(mine, mine, sems.at[t]).wait()
        for o in range(terms):
            block = blocks[t * classes + table[3 * asked + o]].reshape(size, size)
            lifted = jnp.dot(left[t, o], block, preferred_element_type=jnp.float32).astype(jnp.bfloat16)
            term = lax.dot_general(
                lifted, right[t, o], (((1,), (1,)), ((), ())), preferred_element_type=jnp.float32
            )
            if o == 0:
                total[...] = term
            else:
                total[...] += term
        keep[t] = total[pl.ds(pl.multiple_of(me * rows, rows), rows), :]
        for k in range(1, op_size):
            other = lax.rem(me + k, op_size)
            send[k - 1, t] = total[pl.ds(pl.multiple_of(other * rows, rows), rows), :].astype(jnp.bfloat16)


def shards(wave, left_ops, right_ops, owner_map, local_map, op_class):
    op_size = lax.axis_size("op")
    targets, terms, size, _ = left_ops.shape
    sec_dev, rows, _ = wave.shape
    classes = owner_map.shape[1]
    chunks = 2
    part = sec_dev // chunks

    sources = []
    for i in range(chunks):
        gathered = lax.all_gather(wave[i * part : (i + 1) * part], ("chip", "op"))
        sources += [gathered, lax.ppermute(gathered, "core", [(0, 1), (1, 0)])]

    owner, local = owner_map.reshape(-1), local_map.reshape(-1)
    table = jnp.concatenate(
        [
            2 * (local // part) + (owner + lax.axis_index("core")) % 2,
            owner // 2,
            local % part,
            op_class,
            lax.axis_index("op").reshape(1),
        ]
    ).astype(jnp.int32)

    whole = pl.BlockSpec(memory_space=pltpu.VMEM)
    keep, send = pl.pallas_call(
        functools.partial(products, (targets, terms, classes, op_size, len(sources))),
        in_specs=[pl.BlockSpec(memory_space=pltpu.SMEM)]
        + [pl.BlockSpec(memory_space=pl.ANY)] * len(sources)
        + [whole, whole],
        out_specs=[whole, whole],
        out_shape=[
            jax.ShapeDtypeStruct((targets, rows, size), jnp.float32),
            jax.ShapeDtypeStruct((op_size - 1, targets, rows, size), jnp.bfloat16),
        ],
        scratch_shapes=[
            pltpu.VMEM((targets * classes, op_size, rows, size), jnp.bfloat16),
            pltpu.VMEM((size, size), jnp.float32),
            pltpu.SemaphoreType.DMA((targets,)),
        ],
        compiler_params=pltpu.CompilerParams(vmem_limit_bytes=32 * 1024 * 1024),
        cost_estimate=pl.CostEstimate(
            flops=4 * targets * terms * size**3,
            bytes_accessed=6 * targets * terms * size**2,
            transcendentals=0,
        ),
    )(table, *sources, left_ops, right_ops)
    for k in range(1, op_size):
        turn = [(p, (p + k) % op_size) for p in range(op_size)]
        keep = keep + lax.ppermute(send[k - 1], "op", turn).astype(jnp.float32)
    return keep.astype(jnp.bfloat16)


def solution(mesh):
    sec_size, op_size = mesh.shape["sec"], mesh.shape["op"]
    split = Mesh(mesh.devices.reshape(sec_size // 2, 2, op_size), ("chip", "core", "op"))
    sec = ("chip", "core")
    in_specs = (
        P(sec, "op", None),
        P(sec, "op", None, None),
        P(sec, "op", None, None),
        P(sec, None),
        P(sec, None),
        P("op"),
    )
    out_specs = P(sec, "op", None)
    return jax.shard_map(shards, mesh=split, in_specs=in_specs, out_specs=out_specs, check_vma=False)
```

```python
import functools

import jax
import jax.numpy as jnp
from jax import lax
from jax.experimental import pallas as pl
from jax.experimental.pallas import tpu as pltpu
from jax.sharding import Mesh, PartitionSpec as P


def ring_position(chip, chips):
    return jnp.where(lax.rem(chip, 2) == 0, lax.div(chip, 2), chips - 1 - lax.div(chip, 2))


def products(sizes, *refs):
    targets, terms, classes, op_size, chips = sizes
    half = chips // 2
    units = [refs[i * op_size : (i + 1) * op_size] for i in range(2 * chips)]
    left, right, *asked, keep, send = refs[2 * chips * op_size :][:7]
    owner_map, local_map, op_class, blocks, lefts, rights, block_sems, op_sems, sems = refs[-9:]
    size = left.shape[-1]
    rows = size // op_size
    me, core = lax.axis_index("op"), lax.axis_index("core")
    place = ring_position(lax.axis_index("chip"), chips)

    def fetch(unit, sector, t, r):
        for j, source in enumerate(unit):
            pltpu.make_async_copy(
                source.at[sector], blocks.at[r, lax.rem(me + j, op_size)], block_sems.at[t]
            ).start()

    def pick(index, low, high, sector, t, r):
        if high - low == 1:
            fetch(units[low], sector, t, r)
            return
        middle = (low + high) // 2

        @pl.when(index < middle)
        def _():
            pick(index, low, middle, sector, t, r)

        @pl.when(index >= middle)
        def _():
            pick(index, middle, high, sector, t, r)

    def loads(t):
        return (
            pltpu.make_async_copy(left.at[t], lefts.at[t], op_sems.at[0, t]),
            pltpu.make_async_copy(right.at[t], rights.at[t], op_sems.at[1, t]),
        )

    tables = [
        pltpu.make_async_copy(source, target, sems.at[i])
        for i, (source, target) in enumerate(zip(asked, (owner_map, local_map, op_class)))
    ]
    for table in tables:
        table.start()
    for table in tables:
        table.wait()

    @pl.loop(0, targets)
    def _(t):
        for load in loads(t):
            load.start()

        @pl.loop(0, classes)
        def _(c):
            owner = owner_map[t, c]
            offset = lax.rem(ring_position(lax.div(owner, 2), chips) + chips - place, chips)
            distance = jnp.minimum(offset, chips - offset)
            same = lax.rem(owner + core, 2)
            near = jnp.where(offset > half, 0, 1) == core
            inner = jnp.where(near, same, 2 + same)
            index = jnp.where(
                distance == 0,
                same,
                jnp.where(distance == half, 4 * half - 2 + same, 4 * distance - 2 + inner),
            )
            pick(index, 0, 2 * chips, local_map[t, c], t, t * classes + c)

    @pl.loop(0, targets)
    def _(t):
        mine = blocks.at[pl.ds(t * classes, classes)]
        pltpu.make_async_copy(mine, mine, block_sems.at[t]).wait()
        for load in loads(t):
            load.wait()
        total = jnp.zeros((size, size), jnp.float32)
        for o in range(terms):
            block = blocks[t * classes + op_class[o]].reshape(size, size)
            lifted = jnp.dot(lefts[t, o], block, preferred_element_type=jnp.float32).astype(jnp.bfloat16)
            total += lax.dot_general(
                lifted, rights[t, o], (((1,), (1,)), ((), ())), preferred_element_type=jnp.float32
            )
        for j in range(op_size):
            part = total[j * rows : (j + 1) * rows]
            away = lax.rem(j + op_size - me, op_size)

            @pl.when(away == 0)
            def _():
                keep[t] = part

            @pl.when(away != 0)
            def _():
                send[away - 1, t] = part.astype(jnp.bfloat16)


def shards(wave, left_ops, right_ops, owner_map, local_map, op_class):
    chips, op_size = lax.axis_size("chip"), lax.axis_size("op")
    targets, terms, size, _ = left_ops.shape
    sec_dev, rows, _ = wave.shape
    classes = owner_map.shape[1]
    half = chips // 2
    ring = list(range(0, chips, 2)) + list(range(1, chips, 2))[::-1]

    def hop(x):
        pairs = [
            (2 * ring[i] + core, 2 * ring[(i + 1 - 2 * core) % chips] + core)
            for i in range(chips)
            for core in range(2)
        ]
        return lax.ppermute(x, ("chip", "core"), pairs)

    def swap(x):
        return lax.ppermute(x, "core", [(0, 1), (1, 0)])

    def across(x):
        return [
            lax.ppermute(x, "op", [((q + j) % op_size, q) for q in range(op_size)])
            for j in range(1, op_size)
        ]

    own, other, beside = wave, swap(wave), across(wave)
    units = [[own] + beside, [other] + [swap(x) for x in beside]]
    for _ in range(1, half):
        own, other, beside = hop(own), hop(other), [hop(x) for x in beside]
        first, second = [own] + beside, [other] + across(other)
        units += [first, second, [swap(x) for x in second], [swap(x) for x in first]]
    own = hop(own)
    last = [own] + across(own)
    units += [last, [swap(x) for x in last]]
    arrays = [x for unit in units for x in unit]

    whole = pl.BlockSpec(memory_space=pltpu.VMEM)
    stored = pl.BlockSpec(memory_space=pltpu.HBM)
    apart = pl.BlockSpec(memory_space=pl.ANY)
    keep, send = pl.pallas_call(
        functools.partial(products, (targets, terms, classes, op_size, chips)),
        in_specs=[stored] + [apart] * (len(arrays) - 1) + [stored] * 5,
        out_specs=[whole, whole],
        out_shape=[
            jax.ShapeDtypeStruct((targets, rows, size), jnp.float32),
            jax.ShapeDtypeStruct((op_size - 1, targets, rows, size), jnp.bfloat16),
        ],
        scratch_shapes=[
            pltpu.SMEM(owner_map.shape, jnp.int32),
            pltpu.SMEM(local_map.shape, jnp.int32),
            pltpu.SMEM(op_class.shape, jnp.int32),
            pltpu.VMEM((targets * classes, op_size, rows, size), jnp.bfloat16),
            pltpu.VMEM(left_ops.shape, jnp.bfloat16),
            pltpu.VMEM(right_ops.shape, jnp.bfloat16),
            pltpu.SemaphoreType.DMA((targets,)),
            pltpu.SemaphoreType.DMA((2, targets)),
            pltpu.SemaphoreType.DMA((3,)),
        ],
        compiler_params=pltpu.CompilerParams(vmem_limit_bytes=32 * 1024 * 1024),
        cost_estimate=pl.CostEstimate(
            flops=4 * targets * terms * size**3,
            bytes_accessed=6 * targets * terms * size**2,
            transcendentals=0,
        ),
    )(*arrays, left_ops, right_ops, owner_map, local_map, op_class)
    for k in range(1, op_size):
        turn = [(p, (p + k) % op_size) for p in range(op_size)]
        keep = keep + lax.ppermute(send[k - 1], "op", turn).astype(jnp.float32)
    return keep.astype(jnp.bfloat16)


def solution(mesh):
    sec_size, op_size = mesh.shape["sec"], mesh.shape["op"]
    split = Mesh(mesh.devices.reshape(sec_size // 2, 2, op_size), ("chip", "core", "op"))
    sec = ("chip", "core")
    in_specs = (
        P(sec, "op", None),
        P(sec, "op", None, None),
        P(sec, "op", None, None),
        P(sec, None),
        P(sec, None),
        P("op"),
    )
    out_specs = P(sec, "op", None)
    return jax.shard_map(shards, mesh=split, in_specs=in_specs, out_specs=out_specs, check_vma=False)
```

```python
import functools

import jax
import jax.numpy as jnp
from jax import lax
from jax.experimental import pallas as pl
from jax.experimental.pallas import tpu as pltpu
from jax.sharding import Mesh, PartitionSpec as P

LATE = 2


def ring_position(chip, chips):
    return jnp.where(lax.rem(chip, 2) == 0, lax.div(chip, 2), chips - 1 - lax.div(chip, 2))


def unit_of(owner, chips):
    half = chips // 2
    core = lax.axis_index("core")
    place = ring_position(lax.axis_index("chip"), chips)
    offset = lax.rem(ring_position(lax.div(owner, 2), chips) + chips - place, chips)
    distance = jnp.minimum(offset, chips - offset)
    other = lax.rem(owner + core, 2)
    near = jnp.where(offset > half, 0, 1) == core
    between = 4 * distance - 2 + jnp.where(near, other, 2 + other)
    ends = jnp.where(distance == 0, other, 4 * half - 2 + other)
    return jnp.where((distance == 0) | (distance == half), ends, between)


def fetch(unit, sector, blocks, r, sem):
    op_size = len(unit)
    me = lax.axis_index("op")
    for j, source in enumerate(unit):
        pltpu.make_async_copy(source.at[sector], blocks.at[r, lax.rem(me + j, op_size)], sem).start()


def pick(units, index, low, high, sector, blocks, r, sem):
    if high - low == 1:
        fetch(units[low], sector, blocks, r, sem)
        return
    middle = (low + high) // 2

    @pl.when(index < middle)
    def _():
        pick(units, index, low, middle, sector, blocks, r, sem)

    @pl.when(index >= middle)
    def _():
        pick(units, index, middle, high, sector, blocks, r, sem)


def early_kernel(sizes, owner_map, local_map, op_class, *refs):
    targets, terms, classes, op_size, chips = sizes
    early = 2 * chips - LATE
    units = [refs[i * op_size : (i + 1) * op_size] for i in range(early)]
    left, right, lefts, rights, blocks, table_out, table, block_sems, op_sems, table_sem = refs[
        early * op_size :
    ]
    loads = [
        pltpu.make_async_copy(source.at[t], target.at[t], op_sems.at[i, t])
        for t in range(targets)
        for i, (source, target) in enumerate(((left, lefts), (right, rights)))
    ]
    for load in loads:
        load.start()

    @pl.loop(0, targets)
    def _(t):
        @pl.loop(0, classes)
        def _(c):
            r = t * classes + c
            index = unit_of(owner_map[t, c], chips)
            table[0, r] = index
            table[1, r] = local_map[t, c]

            @pl.when(index < early)
            def _():
                pick(units, index, 0, early, local_map[t, c], blocks, r, block_sems.at[r])

    for o in range(terms):
        table[2, o] = op_class[o]
    out = pltpu.make_async_copy(table, table_out, table_sem)
    out.start()
    out.wait()

    @pl.loop(0, targets * classes)
    def _(r):
        @pl.when(table[0, r] < early)
        def _():
            pltpu.make_async_copy(blocks.at[r], blocks.at[r], block_sems.at[r]).wait()

    for load in loads:
        load.wait()


def late_kernel(sizes, first, count, table_in, *refs):
    targets, terms, classes, op_size, chips = sizes
    early = 2 * chips - LATE
    units = [refs[i * op_size : (i + 1) * op_size] for i in range(LATE)]
    lefts, rights, _, keep, send, blocks, table, block_sems, table_sem = refs[LATE * op_size :]
    size = lefts.shape[-1]
    rows = size // op_size
    me = lax.axis_index("op")
    copy = pltpu.make_async_copy(table_in, table, table_sem)
    copy.start()
    copy.wait()
    low, high = first * classes, (first + count) * classes

    @pl.loop(low, high)
    def _(r):
        for i, unit in enumerate(units):

            @pl.when(table[0, r] == early + i)
            def _():
                fetch(unit, table[1, r], blocks, r, block_sems.at[r])

    @pl.loop(0, count)
    def _(step):
        t = first + step

        @pl.loop(0, classes)
        def _(c):
            r = t * classes + c

            @pl.when(table[0, r] >= early)
            def _():
                pltpu.make_async_copy(blocks.at[r], blocks.at[r], block_sems.at[r]).wait()

        lifted = []
        for o in range(terms):
            block = blocks[t * classes + table[2, o]].reshape(size, size)
            lifted.append(
                jnp.dot(lefts[t, o], block, preferred_element_type=jnp.float32).astype(jnp.bfloat16)
            )
        total = lax.dot_general(
            jnp.concatenate(lifted, axis=1),
            jnp.concatenate([rights[t, o] for o in range(terms)], axis=1),
            (((1,), (1,)), ((), ())),
            preferred_element_type=jnp.float32,
        )
        for j in range(op_size):
            part = total[j * rows : (j + 1) * rows]
            away = lax.rem(j + op_size - me, op_size)

            @pl.when(away == 0)
            def _():
                keep[step] = part

            @pl.when(away != 0)
            def _():
                send[away - 1, step] = part.astype(jnp.bfloat16)


def shards(wave, left_ops, right_ops, owner_map, local_map, op_class):
    chips, op_size = lax.axis_size("chip"), lax.axis_size("op")
    targets, terms, size, _ = left_ops.shape
    sec_dev, rows, _ = wave.shape
    classes = owner_map.shape[1]
    half = chips // 2
    ring = list(range(0, chips, 2)) + list(range(1, chips, 2))[::-1]

    def hop(x):
        pairs = [
            (2 * ring[i] + core, 2 * ring[(i + 1 - 2 * core) % chips] + core)
            for i in range(chips)
            for core in range(2)
        ]
        return lax.ppermute(x, ("chip", "core"), pairs)

    def swap(x):
        return lax.ppermute(x, "core", [(0, 1), (1, 0)])

    def across(x):
        return [
            lax.ppermute(x, "op", [((q + j) % op_size, q) for q in range(op_size)])
            for j in range(1, op_size)
        ]

    rules = {}
    crossing_last = False
    reach = dict(own=half, other=half - 1, beside=half - 1 if crossing_last else half, crossed=half - 1)

    @functools.cache
    def arrived(kind, k):
        if k == 0:
            return dict(own=lambda: [wave], other=lambda: [swap(wave)], beside=lambda: across(wave))[kind]()
        x = arrived("other", k) if kind == "crossed" else arrived(kind, k - 1)
        done = []
        for before, shift in rules.get(kind, ()):
            if 1 <= k + shift <= reach[before] and (before, shift) != (kind, 0):
                done += arrived(before, k + shift)
        if done:
            x = [lax.optimization_barrier((y, *done))[0] for y in x]
        if kind == "crossed":
            return across(x[0])
        return [hop(y) for y in x]

    def swapped(arrays, k):
        done = []
        for before, shift in rules.get("swap", ()):
            if 1 <= k + shift <= reach[before]:
                done += arrived(before, k + shift)
        if done:
            arrays = [lax.optimization_barrier((x, *done))[0] for x in arrays]
        return [swap(x) for x in arrays]

    units = []
    for k in range(half + 1):
        first = arrived("own", k) + (
            across(arrived("own", k)[0]) if k == half and crossing_last else arrived("beside", k)
        )
        if k == 0:
            units += [first, arrived("other", 0) + swapped(first[1:], 0)]
        elif k == half:
            units += [first, swapped(first, k)]
        else:
            second = arrived("other", k) + arrived("crossed", k)
            units += [first, second, swapped(second, k), swapped(first, k)]
    arrays = [x for unit in units for x in unit]
    split = len(arrays) - LATE * op_size

    sizes = (targets, terms, classes, op_size, chips)
    asked = targets * classes
    whole = pl.BlockSpec(memory_space=pltpu.VMEM)
    scalars = pl.BlockSpec(memory_space=pltpu.SMEM)
    apart = pl.BlockSpec(memory_space=pl.ANY)
    block_shape = (asked, op_size, rows, size)
    table_shape = (8, 128)
    lefts, rights, blocks, table = pl.pallas_call(
        functools.partial(early_kernel, sizes),
        in_specs=[scalars] * 3 + [apart] * (split + 2),
        out_specs=[whole] * 4,
        out_shape=[
            jax.ShapeDtypeStruct(left_ops.shape, jnp.bfloat16),
            jax.ShapeDtypeStruct(right_ops.shape, jnp.bfloat16),
            jax.ShapeDtypeStruct(block_shape, jnp.bfloat16),
            jax.ShapeDtypeStruct(table_shape, jnp.int32),
        ],
        scratch_shapes=[
            pltpu.SMEM(table_shape, jnp.int32),
            pltpu.SemaphoreType.DMA((asked,)),
            pltpu.SemaphoreType.DMA((2, targets)),
            pltpu.SemaphoreType.DMA,
        ],
        compiler_params=pltpu.CompilerParams(vmem_limit_bytes=24 * 1024 * 1024),
        cost_estimate=pl.CostEstimate(
            flops=0,
            bytes_accessed=2 * (left_ops.size + right_ops.size + asked * size**2),
            transcendentals=0,
        ),
    )(owner_map, local_map, op_class, *arrays[:split], left_ops, right_ops)

    results = []
    for first in range(0, targets, 6):
        count = min(6, targets - first)
        keep, send, blocks = pl.pallas_call(
            functools.partial(late_kernel, sizes, first, count),
            in_specs=[whole] + [apart] * (LATE * op_size) + [whole] * 3,
            out_specs=[whole] * 3,
            out_shape=[
                jax.ShapeDtypeStruct((count, rows, size), jnp.float32),
                jax.ShapeDtypeStruct((op_size - 1, count, rows, size), jnp.bfloat16),
                jax.ShapeDtypeStruct(block_shape, jnp.bfloat16),
            ],
            input_output_aliases={1 + LATE * op_size + 2: 2},
            scratch_shapes=[
                pltpu.SMEM(table_shape, jnp.int32),
                pltpu.SemaphoreType.DMA((asked,)),
                pltpu.SemaphoreType.DMA,
            ],
            compiler_params=pltpu.CompilerParams(vmem_limit_bytes=24 * 1024 * 1024),
            cost_estimate=pl.CostEstimate(
                flops=4 * count * terms * size**3,
                bytes_accessed=4 * count * terms * size**2,
                transcendentals=0,
            ),
        )(table, *arrays[split:], lefts, rights, blocks)
        for k in range(1, op_size):
            turn = [(p, (p + k) % op_size) for p in range(op_size)]
            keep = keep + lax.ppermute(send[k - 1], "op", turn).astype(jnp.float32)
        results.append(keep.astype(jnp.bfloat16))
    return jnp.concatenate(results)


def solution(mesh):
    sec_size, op_size = mesh.shape["sec"], mesh.shape["op"]
    split = Mesh(mesh.devices.reshape(sec_size // 2, 2, op_size), ("chip", "core", "op"))
    sec = ("chip", "core")
    in_specs = (
        P(sec, "op", None),
        P(sec, "op", None, None),
        P(sec, "op", None, None),
        P(sec, None),
        P(sec, None),
        P("op"),
    )
    out_specs = P(sec, "op", None)
    return jax.shard_map(shards, mesh=split, in_specs=in_specs, out_specs=out_specs, check_vma=False)
```

```python
import functools

import jax
import jax.numpy as jnp
from jax import lax
from jax.experimental import pallas as pl
from jax.experimental.pallas import tpu as pltpu
from jax.sharding import Mesh, PartitionSpec as P

HERE, HERE_AT, AWAY, AWAY_AT, SECTOR, CLASS, LATER = range(7)
TABLE = (8, 128)
VMEM_BYTES = 24 * 1024 * 1024


def ring_position(chip, chips):
    return jnp.where(lax.rem(chip, 2) == 0, lax.div(chip, 2), chips - 1 - lax.div(chip, 2))


def table_kernel(sizes, owner_map, local_map, op_class, wave, table_out, wave_out, table, unit_of, sems):
    targets, terms, classes, op_size, chips = sizes
    half = chips // 2
    asked = targets * classes
    core = lax.axis_index("core")
    place = ring_position(lax.axis_index("chip"), chips)
    wave_copy = pltpu.make_async_copy(wave, wave_out, sems.at[0])
    wave_copy.start()

    @pl.loop(0, targets)
    def _(t):
        @pl.loop(0, classes)
        def _(c):
            r = t * classes + c
            owner = owner_map[t, c]
            owner_core = lax.rem(owner, 2)
            offset = lax.rem(ring_position(lax.div(owner, 2), chips) + chips - place, chips)
            distance = jnp.minimum(offset, chips - offset)
            end = (distance == 0) | (distance == half)
            holder = jnp.where(end, owner_core, jnp.where(offset > half, 0, 1))
            unit = jnp.where(distance == 0, 0, 2 * distance - jnp.where(owner_core == holder, 1, 0))
            away = jnp.where(holder == core, 0, 1)
            unit_of[r] = unit + away * chips
            table[SECTOR, r] = local_map[t, c]
            table[LATER, r] = away

    for o in range(terms):
        table[CLASS, o] = op_class[o]

    def listed(order, start, shift):
        def unit_step(u, filled):
            table[start, u] = filled

            def request_step(r, filled):
                match = unit_of[r] == u + shift

                @pl.when(match)
                def _():
                    table[order, filled] = r

                return filled + match.astype(jnp.int32)

            return lax.fori_loop(0, asked, request_step, filled)

        table[start, chips] = lax.fori_loop(0, chips, unit_step, jnp.int32(0))

    listed(HERE, HERE_AT, 0)
    listed(AWAY, AWAY_AT, chips)
    out = pltpu.make_async_copy(table, table_out, sems.at[1])
    out.start()
    out.wait()
    wave_copy.wait()


def fetch(unit, sector, target, sem):
    op_size = len(unit)
    me = lax.axis_index("op")
    for j, source in enumerate(unit):
        pltpu.make_async_copy(source.at[sector], target.at[lax.rem(me + j, op_size)], sem).start()


def stage_kernel(sizes, low, high, loading, table_in, asked_in, *refs):
    targets, terms, classes, op_size, chips = sizes
    count = high - low
    units = [refs[i * op_size : (i + 1) * op_size] for i in range(count)]
    refs = refs[count * op_size :]
    blocks, sent, table, theirs, block_sems, sent_sems, sems = refs[-7:]
    tables = [
        pltpu.make_async_copy(table_in, table, sems.at[0]),
        pltpu.make_async_copy(asked_in, theirs, sems.at[1]),
    ]
    for copy in tables:
        copy.start()
    loads = []
    if loading:
        left, right, lefts, rights = refs[:4]
        loads = [
            pltpu.make_async_copy(left, lefts, sems.at[2]),
            pltpu.make_async_copy(right, rights, sems.at[3]),
        ]
    for load in loads:
        load.start()
    for copy in tables:
        copy.wait()
    skipped = theirs[AWAY_AT, low]
    for u, unit in enumerate(units, low):

        @pl.loop(theirs[AWAY_AT, u], theirs[AWAY_AT, u + 1])
        def _(i):
            slot = i - skipped
            fetch(unit, theirs[SECTOR, theirs[AWAY, i]], sent.at[slot], sent_sems.at[slot])

    for u, unit in enumerate(units, low):

        @pl.loop(table[HERE_AT, u], table[HERE_AT, u + 1])
        def _(i):
            r = table[HERE, i]
            fetch(unit, table[SECTOR, r], blocks.at[r], block_sems.at[r])

    @pl.loop(0, theirs[AWAY_AT, high] - skipped)
    def _(slot):
        pltpu.make_async_copy(sent.at[slot], sent.at[slot], sent_sems.at[slot]).wait()

    @pl.loop(table[HERE_AT, low], table[HERE_AT, high])
    def _(i):
        r = table[HERE, i]
        pltpu.make_async_copy(blocks.at[r], blocks.at[r], block_sems.at[r]).wait()

    for load in loads:
        load.wait()


def product_kernel(sizes, bounds, first, count, table_in, *refs):
    targets, terms, classes, op_size, chips = sizes
    stages = len(bounds) - 1
    received = refs[:stages]
    lefts, rights, _, keep, send, blocks, table, block_sems, table_sem = refs[stages:]
    size = lefts.shape[-1]
    rows = size // op_size
    me = lax.axis_index("op")
    copy = pltpu.make_async_copy(table_in, table, table_sem)
    copy.start()
    copy.wait()
    first_asked, last_asked = first * classes, (first + count) * classes
    for source, low, high in zip(received, bounds[:-1], bounds[1:]):
        skipped = table[AWAY_AT, low]

        @pl.loop(skipped, table[AWAY_AT, high])
        def _(i):
            r = table[AWAY, i]

            @pl.when((r >= first_asked) & (r < last_asked))
            def _():
                pltpu.make_async_copy(source.at[i - skipped], blocks.at[r], block_sems.at[r]).start()

    @pl.loop(0, count)
    def _(step):
        t = first + step

        @pl.loop(0, classes)
        def _(c):
            r = t * classes + c

            @pl.when(table[LATER, r] == 1)
            def _():
                pltpu.make_async_copy(blocks.at[r], blocks.at[r], block_sems.at[r]).wait()

        lifted = []
        for o in range(terms):
            block = blocks[t * classes + table[CLASS, o]].reshape(size, size)
            lifted.append(
                jnp.dot(lefts[t, o], block, preferred_element_type=jnp.float32).astype(jnp.bfloat16)
            )
        total = lax.dot_general(
            jnp.concatenate(lifted, axis=1),
            jnp.concatenate([rights[t, o] for o in range(terms)], axis=1),
            (((1,), (1,)), ((), ())),
            preferred_element_type=jnp.float32,
        )
        for j in range(op_size):
            part = total[j * rows : (j + 1) * rows]
            distance = lax.rem(j + op_size - me, op_size)

            @pl.when(distance == 0)
            def _():
                keep[step] = part

            @pl.when(distance != 0)
            def _():
                send[distance - 1, step] = part.astype(jnp.bfloat16)


def shards(wave, left_ops, right_ops, owner_map, local_map, op_class):
    chips, op_size = lax.axis_size("chip"), lax.axis_size("op")
    targets, terms, size, _ = left_ops.shape
    sec_dev, rows, _ = wave.shape
    classes = owner_map.shape[1]
    half = chips // 2
    asked = targets * classes
    sizes = (targets, terms, classes, op_size, chips)
    most = max(2, (asked + 2 * chips - 1) // (2 * chips) + 1)
    ring = list(range(0, chips, 2)) + list(range(1, chips, 2))[::-1]

    def hop(x):
        pairs = [
            (2 * ring[i] + core, 2 * ring[(i + 1 - 2 * core) % chips] + core)
            for i in range(chips)
            for core in range(2)
        ]
        return lax.ppermute(x, ("chip", "core"), pairs)

    def swap(x):
        return lax.ppermute(x, "core", [(0, 1), (1, 0)])

    def across(x):
        return [
            lax.ppermute(x, "op", [((q + j) % op_size, q) for q in range(op_size)])
            for j in range(1, op_size)
        ]

    whole = pl.BlockSpec(memory_space=pltpu.VMEM)
    scalars = pl.BlockSpec(memory_space=pltpu.SMEM)
    apart = pl.BlockSpec(memory_space=pl.ANY)
    limit = pltpu.CompilerParams(vmem_limit_bytes=VMEM_BYTES)
    table, wave_near = pl.pallas_call(
        functools.partial(table_kernel, sizes),
        in_specs=[scalars] * 3 + [apart],
        out_specs=[whole] * 2,
        out_shape=[
            jax.ShapeDtypeStruct(TABLE, jnp.int32),
            jax.ShapeDtypeStruct(wave.shape, wave.dtype),
        ],
        scratch_shapes=[
            pltpu.SMEM(TABLE, jnp.int32),
            pltpu.SMEM((asked,), jnp.int32),
            pltpu.SemaphoreType.DMA((2,)),
        ],
        compiler_params=limit,
        cost_estimate=pl.CostEstimate(flops=0, bytes_accessed=0, transcendentals=0),
    )(owner_map, local_map, op_class, wave)
    rules = {'beside': [('other', 0)], 'other': [('crossed', -2)]}

    @functools.cache
    def arrived(kind, k):
        if k == 0:
            return dict(own=lambda: [wave], other=lambda: [swap(wave)], beside=lambda: across(wave))[kind]()
        x = arrived("other", k) if kind == "crossed" else arrived(kind, k - 1)
        done = []
        for before, shift in rules.get(kind, ()):
            most_hops = half - 1 if before in ("other", "crossed") else half
            if 1 <= k + shift <= most_hops:
                done += arrived(before, k + shift)
        if done:
            x = [lax.optimization_barrier((y, *done))[0] for y in x]
        if (kind, k) == ('beside', 1):
            x = [lax.optimization_barrier((y, table))[0] for y in x]
        if kind == "crossed":
            return across(x[0])
        return [hop(y) for y in x]

    their_table = swap(table)
    units = [[wave_near] + arrived("beside", 0)]
    for k in range(1, half):
        units += [arrived("own", k) + arrived("beside", k), arrived("other", k) + arrived("crossed", k)]
    units.append(arrived("own", half) + arrived("beside", half))

    bounds = [0, chips - 3, chips]
    block_shape = (asked, op_size, rows, size)
    blocks_out = jax.ShapeDtypeStruct(block_shape, jnp.bfloat16)
    received = []
    for low, high in zip(bounds[:-1], bounds[1:]):
        arrays = [x for unit in units[low:high] for x in unit]
        loading = low == 0
        if loading:
            tied = [x for kind, k in () for x in arrived(kind, k)]
            if tied:
                arrays[0] = lax.optimization_barrier((arrays[0], *tied))[0]
        slots = min(asked, (high - low) * most)
        operands = [table, their_table, *arrays] + ([left_ops, right_ops] if loading else [blocks])
        operators_out = [
            jax.ShapeDtypeStruct(left_ops.shape, jnp.bfloat16),
            jax.ShapeDtypeStruct(right_ops.shape, jnp.bfloat16),
        ]
        outs = pl.pallas_call(
            functools.partial(stage_kernel, sizes, low, high, loading),
            in_specs=[whole] * 2 + [apart] * len(arrays) + ([apart] * 2 if loading else [whole]),
            out_specs=[whole] * (4 if loading else 2),
            out_shape=(operators_out if loading else [])
            + [blocks_out, jax.ShapeDtypeStruct((slots,) + block_shape[1:], jnp.bfloat16)],
            input_output_aliases={} if loading else {len(operands) - 1: 0},
            scratch_shapes=[
                pltpu.SMEM(TABLE, jnp.int32),
                pltpu.SMEM(TABLE, jnp.int32),
                pltpu.SemaphoreType.DMA((asked,)),
                pltpu.SemaphoreType.DMA((slots,)),
                pltpu.SemaphoreType.DMA((4,)),
            ],
            compiler_params=limit,
            cost_estimate=pl.CostEstimate(
                flops=0,
                bytes_accessed=sum(2 * x.size for x in operands[2:]),
                transcendentals=0,
            ),
        )(*operands)
        if loading:
            lefts, rights = outs[:2]
        blocks, sent = outs[-2:]
        received.append(swap(sent))

    results = []
    for first in range(0, targets, 6):
        count = min(6, targets - first)
        keep, send, blocks = pl.pallas_call(
            functools.partial(product_kernel, sizes, bounds, first, count),
            in_specs=[whole] + [apart] * len(received) + [whole] * 3,
            out_specs=[whole] * 3,
            out_shape=[
                jax.ShapeDtypeStruct((count, rows, size), jnp.float32),
                jax.ShapeDtypeStruct((op_size - 1, count, rows, size), jnp.bfloat16),
                blocks_out,
            ],
            input_output_aliases={len(received) + 3: 2},
            scratch_shapes=[
                pltpu.SMEM(TABLE, jnp.int32),
                pltpu.SemaphoreType.DMA((asked,)),
                pltpu.SemaphoreType.DMA,
            ],
            compiler_params=limit,
            cost_estimate=pl.CostEstimate(
                flops=4 * count * terms * size**3,
                bytes_accessed=4 * count * terms * size**2,
                transcendentals=0,
            ),
        )(table, *received, lefts, rights, blocks)
        for k in range(1, op_size):
            turn = [(p, (p + k) % op_size) for p in range(op_size)]
            keep = keep + lax.ppermute(send[k - 1], "op", turn).astype(jnp.float32)
        results.append(keep.astype(jnp.bfloat16))
    return jnp.concatenate(results)


def solution(mesh):
    sec_size, op_size = mesh.shape["sec"], mesh.shape["op"]
    split = Mesh(mesh.devices.reshape(sec_size // 2, 2, op_size), ("chip", "core", "op"))
    sec = ("chip", "core")
    in_specs = (
        P(sec, "op", None),
        P(sec, "op", None, None),
        P(sec, "op", None, None),
        P(sec, None),
        P(sec, None),
        P("op"),
    )
    out_specs = P(sec, "op", None)
    return jax.shard_map(shards, mesh=split, in_specs=in_specs, out_specs=out_specs, check_vma=False)
```

```python
import functools

import jax
import jax.numpy as jnp
from jax import lax
from jax.experimental import pallas as pl
from jax.experimental.pallas import tpu as pltpu
from jax.sharding import Mesh, PartitionSpec as P

ORDER, START, SECTOR, CLASS, LATER = range(5)
TABLE = (8, 128)
VMEM_BYTES = 24 * 1024 * 1024


def ring_position(chip, chips):
    return jnp.where(lax.rem(chip, 2) == 0, lax.div(chip, 2), chips - 1 - lax.div(chip, 2))


def table_kernel(sizes, early, owner_map, local_map, op_class, *refs):
    targets, terms, classes, op_size, chips = sizes
    half = chips // 2
    core = lax.axis_index("core")
    place = ring_position(lax.axis_index("chip"), chips)
    left, right, table_out, lefts, rights, table, unit_of, filled, sems = refs
    loads = [
        pltpu.make_async_copy(left, lefts, sems.at[0]),
        pltpu.make_async_copy(right, rights, sems.at[1]),
    ]
    for load in loads:
        load.start()

    @pl.loop(0, 2 * chips)
    def _(u):
        filled[u] = 0

    @pl.loop(0, targets)
    def _(t):
        @pl.loop(0, classes)
        def _(c):
            r = t * classes + c
            owner = owner_map[t, c]
            owner_core = owner & 1
            chip = owner >> 1
            position = jnp.where((chip & 1) == 0, chip >> 1, chips - 1 - (chip >> 1))
            offset = position - place
            offset = jnp.where(offset < 0, offset + chips, offset)
            distance = jnp.minimum(offset, chips - offset)
            end = (distance == 0) | (distance == half)
            holder = jnp.where(end, owner_core, jnp.where(offset > half, 0, 1))
            unit = jnp.where(distance == 0, 0, 2 * distance - jnp.where(owner_core == holder, 1, 0))
            away = jnp.where(holder == core, 0, 1)
            slot = unit + away * chips
            unit_of[r] = slot
            filled[slot] = filled[slot] + 1
            table[SECTOR, r] = local_map[t, c]
            table[LATER, r] = jnp.where((away == 1) | (unit >= early), 1, 0)

    for o in range(terms):
        table[CLASS, o] = op_class[o]

    def place_unit(u, at):
        table[START, u] = at
        count = filled[u]
        filled[u] = at
        return at + count

    table[START, 2 * chips] = lax.fori_loop(0, 2 * chips, place_unit, jnp.int32(0))

    @pl.loop(0, targets * classes)
    def _(r):
        u = unit_of[r]
        at = filled[u]
        table[ORDER, at] = r
        filled[u] = at + 1

    out = pltpu.make_async_copy(table, table_out, sems.at[2])
    out.start()
    for copy in [out] + loads:
        copy.wait()


def fetch(unit, sector, target, sem):
    op_size = len(unit)
    me = lax.axis_index("op")
    for j, source in enumerate(unit):
        pltpu.make_async_copy(source.at[sector], target.at[lax.rem(me + j, op_size)], sem).start()


def stage_kernel(sizes, low, high, asked_in, table_in, *refs):
    targets, terms, classes, op_size, chips = sizes
    count = high - low
    units = [refs[i * op_size : (i + 1) * op_size] for i in range(count)]
    refs = refs[count * op_size :]
    if low == 0:
        blocks = refs[0]
    sent, table, theirs, block_sems, sent_sems, sems = refs[-6:]
    copies = [pltpu.make_async_copy(asked_in, theirs, sems.at[0])]
    if low == 0:
        copies.append(pltpu.make_async_copy(table_in, table, sems.at[1]))
    for copy in copies:
        copy.start()
    for copy in copies:
        copy.wait()
    skipped = theirs[START, chips + low]
    for u, unit in enumerate(units, low):

        @pl.loop(theirs[START, chips + u], theirs[START, chips + u + 1])
        def _(i):
            slot = i - skipped
            fetch(unit, theirs[SECTOR, theirs[ORDER, i]], sent.at[slot], sent_sems.at[slot])

        if low == 0:

            @pl.loop(table[START, u], table[START, u + 1])
            def _(i):
                r = table[ORDER, i]
                fetch(unit, table[SECTOR, r], blocks.at[r], block_sems.at[r])

    @pl.loop(0, theirs[START, chips + high] - skipped)
    def _(slot):
        pltpu.make_async_copy(sent.at[slot], sent.at[slot], sent_sems.at[slot]).wait()

    if low == 0:

        @pl.loop(0, table[START, high])
        def _(i):
            r = table[ORDER, i]
            pltpu.make_async_copy(blocks.at[r], blocks.at[r], block_sems.at[r]).wait()


def product_kernel(sizes, bounds, first, count, table_in, *refs):
    targets, terms, classes, op_size, chips = sizes
    stages, early = len(bounds) - 1, bounds[1]
    received, refs = refs[:stages], refs[stages:]
    units = [refs[i * op_size : (i + 1) * op_size] for i in range(chips - early)]
    refs = refs[(chips - early) * op_size :]
    lefts, rights, _, keep, send, blocks, table, block_sems, table_sem = refs
    size = lefts.shape[-1]
    rows = size // op_size
    me = lax.axis_index("op")
    copy = pltpu.make_async_copy(table_in, table, table_sem)
    copy.start()
    copy.wait()

    def each(low, high, body):
        @pl.loop(table[START, low], table[START, high])
        def _(i):
            r = table[ORDER, i]
            if count == targets:
                body(i, r)
            else:

                @pl.when((r >= first * classes) & (r < (first + count) * classes))
                def _():
                    body(i, r)

    for u, unit in enumerate(units, early):

        def from_unit(i, r):
            fetch(unit, table[SECTOR, r], blocks.at[r], block_sems.at[r])

        each(u, u + 1, from_unit)
    for source, low, high in zip(received, bounds[:-1], bounds[1:]):
        skipped = table[START, chips + low]

        def from_partner(i, r):
            pltpu.make_async_copy(source.at[i - skipped], blocks.at[r], block_sems.at[r]).start()

        each(chips + low, chips + high, from_partner)

    @pl.loop(0, count)
    def _(step):
        t = first + step

        @pl.loop(0, classes)
        def _(c):
            r = t * classes + c

            @pl.when(table[LATER, r] == 1)
            def _():
                pltpu.make_async_copy(blocks.at[r], blocks.at[r], block_sems.at[r]).wait()

        lifted = []
        for o in range(terms):
            block = blocks[t * classes + table[CLASS, o]].reshape(size, size)
            lifted.append(
                jnp.dot(lefts[t, o], block, preferred_element_type=jnp.float32).astype(jnp.bfloat16)
            )
        total = lax.dot_general(
            jnp.concatenate(lifted, axis=1),
            jnp.concatenate([rights[t, o] for o in range(terms)], axis=1),
            (((1,), (1,)), ((), ())),
            preferred_element_type=jnp.float32,
        )
        for j in range(op_size):
            part = total[j * rows : (j + 1) * rows]
            distance = lax.rem(j + op_size - me, op_size)

            @pl.when(distance == 0)
            def _():
                keep[step] = part

            @pl.when(distance != 0)
            def _():
                send[distance - 1, step] = part.astype(jnp.bfloat16)


def shards(wave, left_ops, right_ops, owner_map, local_map, op_class):
    chips, op_size = lax.axis_size("chip"), lax.axis_size("op")
    targets, terms, size, _ = left_ops.shape
    sec_dev, rows, _ = wave.shape
    classes = owner_map.shape[1]
    half = chips // 2
    asked = targets * classes
    sizes = (targets, terms, classes, op_size, chips)
    bounds = [0, chips - 3, chips]
    most = max(2, (asked + 2 * chips - 1) // (2 * chips) + 1)
    ring = list(range(0, chips, 2)) + list(range(1, chips, 2))[::-1]

    def hop(x):
        pairs = [
            (2 * ring[i] + core, 2 * ring[(i + 1 - 2 * core) % chips] + core)
            for i in range(chips)
            for core in range(2)
        ]
        return lax.ppermute(x, ("chip", "core"), pairs)

    def swap(x):
        return lax.ppermute(x, "core", [(0, 1), (1, 0)])

    def across(x):
        return [
            lax.ppermute(x, "op", [((q + j) % op_size, q) for q in range(op_size)])
            for j in range(1, op_size)
        ]

    whole = pl.BlockSpec(memory_space=pltpu.VMEM)
    scalars = pl.BlockSpec(memory_space=pltpu.SMEM)
    apart = pl.BlockSpec(memory_space=pl.ANY)
    limit = pltpu.CompilerParams(vmem_limit_bytes=VMEM_BYTES)
    table, lefts, rights = pl.pallas_call(
        functools.partial(table_kernel, sizes, bounds[1]),
        in_specs=[scalars] * 3 + [apart] * 2,
        out_specs=[whole] * 3,
        out_shape=[
            jax.ShapeDtypeStruct(TABLE, jnp.int32),
            jax.ShapeDtypeStruct(left_ops.shape, jnp.bfloat16),
            jax.ShapeDtypeStruct(right_ops.shape, jnp.bfloat16),
        ],
        scratch_shapes=[
            pltpu.SMEM(TABLE, jnp.int32),
            pltpu.SMEM((asked,), jnp.int32),
            pltpu.SMEM((2 * chips,), jnp.int32),
            pltpu.SemaphoreType.DMA((3,)),
        ],
        compiler_params=pltpu.CompilerParams(vmem_limit_bytes=36 * 1024 * 1024),
        cost_estimate=pl.CostEstimate(flops=0, bytes_accessed=0, transcendentals=0),
    )(owner_map, local_map, op_class, left_ops, right_ops)
    rules = {'beside': [('crossed', -2)], 'crossed': [('own', -1)], 'own': [('other', -1)]}

    @functools.cache
    def arrived(kind, k):
        if k == 0:
            return dict(own=lambda: [wave], other=lambda: [swap(wave)], beside=lambda: across(wave))[kind]()
        x = arrived("other", k) if kind == "crossed" else arrived(kind, k - 1)
        done = []
        for before, shift in rules.get(kind, ()):
            most_hops = half - 1 if before in ("other", "crossed") else half
            if 1 <= k + shift <= most_hops:
                done += arrived(before, k + shift)
        if done:
            x = [lax.optimization_barrier((y, *done))[0] for y in x]
        if (kind, k) == ('beside', 1):
            x = [lax.optimization_barrier((y, table))[0] for y in x]
        if kind == "crossed":
            return across(x[0])
        return [hop(y) for y in x]

    their_table = swap(table)
    units = [[wave] + arrived("beside", 0)]
    for k in range(1, half):
        units += [arrived("own", k) + arrived("beside", k), arrived("other", k) + arrived("crossed", k)]
    units.append(arrived("own", half) + arrived("beside", half))

    block_shape = (asked, op_size, rows, size)
    blocks_out = jax.ShapeDtypeStruct(block_shape, jnp.bfloat16)
    received = []
    for low, high in zip(bounds[:-1], bounds[1:]):
        arrays = [x for unit in units[low:high] for x in unit]
        slots = min(asked, (high - low) * most)
        sent_out = jax.ShapeDtypeStruct((slots,) + block_shape[1:], jnp.bfloat16)
        outs = [sent_out]
        if low == 0:
            tied = [x for kind, k in (('other', 3),) for x in arrived(kind, k)]
            if tied:
                arrays[0] = lax.optimization_barrier((arrays[0], *tied))[0]
            outs = [blocks_out, sent_out]
        outs = pl.pallas_call(
            functools.partial(stage_kernel, sizes, low, high),
            in_specs=[whole] * 2 + [apart] * len(arrays),
            out_specs=[whole] * len(outs),
            out_shape=outs,
            scratch_shapes=[
                pltpu.SMEM(TABLE, jnp.int32),
                pltpu.SMEM(TABLE, jnp.int32),
                pltpu.SemaphoreType.DMA((asked,)),
                pltpu.SemaphoreType.DMA((slots,)),
                pltpu.SemaphoreType.DMA((2,)),
            ],
            compiler_params=limit,
            cost_estimate=pl.CostEstimate(
                flops=0, bytes_accessed=sum(2 * x.size for x in arrays), transcendentals=0
            ),
        )(their_table, table, *arrays)
        if low == 0:
            blocks = outs[0]
        sent = outs[-1]
        received.append(swap(sent))

    sources = received + [x for unit in units[bounds[1] :] for x in unit]
    results = []
    for first in range(0, targets, 6):
        count = min(6, targets - first)
        keep, send, blocks = pl.pallas_call(
            functools.partial(product_kernel, sizes, bounds, first, count),
            in_specs=[whole] + [apart] * len(sources) + [whole] * 3,
            out_specs=[whole] * 3,
            out_shape=[
                jax.ShapeDtypeStruct((count, rows, size), jnp.float32),
                jax.ShapeDtypeStruct((op_size - 1, count, rows, size), jnp.bfloat16),
                blocks_out,
            ],
            input_output_aliases={len(sources) + 3: 2},
            scratch_shapes=[
                pltpu.SMEM(TABLE, jnp.int32),
                pltpu.SemaphoreType.DMA((asked,)),
                pltpu.SemaphoreType.DMA,
            ],
            compiler_params=limit,
            cost_estimate=pl.CostEstimate(
                flops=4 * count * terms * size**3,
                bytes_accessed=4 * count * terms * size**2,
                transcendentals=0,
            ),
        )(table, *sources, lefts, rights, blocks)
        for k in range(1, op_size):
            turn = [(p, (p + k) % op_size) for p in range(op_size)]
            keep = keep + lax.ppermute(send[k - 1], "op", turn).astype(jnp.float32)
        results.append(keep.astype(jnp.bfloat16))
    return jnp.concatenate(results)


def solution(mesh):
    sec_size, op_size = mesh.shape["sec"], mesh.shape["op"]
    split = Mesh(mesh.devices.reshape(sec_size // 2, 2, op_size), ("chip", "core", "op"))
    sec = ("chip", "core")
    in_specs = (
        P(sec, "op", None),
        P(sec, "op", None, None),
        P(sec, "op", None, None),
        P(sec, None),
        P(sec, None),
        P("op"),
    )
    out_specs = P(sec, "op", None)
    return jax.shard_map(shards, mesh=split, in_specs=in_specs, out_specs=out_specs, check_vma=False)
```

```python
import functools

import jax
import jax.numpy as jnp
from jax import lax
from jax.experimental import pallas as pl
from jax.experimental.pallas import tpu as pltpu
from jax.sharding import Mesh, PartitionSpec as P

ORDER, START, SECTOR, CLASS, LATER = range(5)
TABLE = (8, 128)
LIMITS = dict(table=4, sent=8, load=32, fill=8, product=24)


def ring_position(chip, chips):
    return jnp.where(lax.rem(chip, 2) == 0, lax.div(chip, 2), chips - 1 - lax.div(chip, 2))


def table_kernel(sizes, early, owner_map, local_map, op_class, *refs):
    targets, terms, classes, op_size, chips = sizes
    half = chips // 2
    core = lax.axis_index("core")
    place = ring_position(lax.axis_index("chip"), chips)
    table_out, table, unit_of, filled, sem = refs

    @pl.loop(0, 2 * chips)
    def _(u):
        filled[u] = 0

    @pl.loop(0, targets)
    def _(t):
        @pl.loop(0, classes)
        def _(c):
            r = t * classes + c
            owner = owner_map[t, c]
            owner_core = owner & 1
            chip = owner >> 1
            position = jnp.where((chip & 1) == 0, chip >> 1, chips - 1 - (chip >> 1))
            offset = position - place
            offset = jnp.where(offset < 0, offset + chips, offset)
            distance = jnp.minimum(offset, chips - offset)
            end = (distance == 0) | (distance == half)
            holder = jnp.where(end, owner_core, jnp.where(offset > half, 0, 1))
            unit = jnp.where(distance == 0, 0, 2 * distance - jnp.where(owner_core == holder, 1, 0))
            away = jnp.where(holder == core, 0, 1)
            slot = unit + away * chips
            unit_of[r] = slot
            filled[slot] = filled[slot] + 1
            table[SECTOR, r] = local_map[t, c]
            table[LATER, r] = jnp.where((away == 1) & (unit >= early), 1, 0)

    for o in range(terms):
        table[CLASS, o] = op_class[o]

    def place_unit(u, at):
        table[START, u] = at
        count = filled[u]
        filled[u] = at
        return at + count

    table[START, 2 * chips] = lax.fori_loop(0, 2 * chips, place_unit, jnp.int32(0))

    @pl.loop(0, targets * classes)
    def _(r):
        u = unit_of[r]
        at = filled[u]
        table[ORDER, at] = r
        filled[u] = at + 1

    out = pltpu.make_async_copy(table, table_out, sem)
    out.start()
    out.wait()


def fetch(unit, sector, target, sem):
    op_size = len(unit)
    me = lax.axis_index("op")
    for j, source in enumerate(unit):
        pltpu.make_async_copy(source.at[sector], target.at[lax.rem(me + j, op_size)], sem).start()


def read_table(source, target, sem):
    copy = pltpu.make_async_copy(source, target, sem)
    copy.start()
    copy.wait()


def grouped(refs, size):
    return [refs[i : i + size] for i in range(0, len(refs), size)]


def sent_kernel(sizes, low, high, asked_in, *refs):
    chips, op_size = sizes[4], sizes[3]
    *units, sent, table, slot_sems, sem = refs
    read_table(asked_in, table, sem)
    skipped = table[START, chips + low]
    for u, unit in enumerate(grouped(units, op_size), low):

        @pl.loop(table[START, chips + u], table[START, chips + u + 1])
        def _(i):
            slot = i - skipped
            fetch(unit, table[SECTOR, table[ORDER, i]], sent.at[slot], slot_sems.at[slot])

    @pl.loop(0, table[START, chips + high] - skipped)
    def _(slot):
        pltpu.make_async_copy(sent.at[slot], sent.at[slot], slot_sems.at[slot]).wait()


def fetch_own(units, low, table, blocks, block_sems):
    for u, unit in enumerate(units, low):

        @pl.loop(table[START, u], table[START, u + 1])
        def _(i):
            r = table[ORDER, i]
            fetch(unit, table[SECTOR, r], blocks.at[r], block_sems.at[r])


def fetch_received(received, first, last, table, blocks, block_sems):
    skipped = table[START, first]

    @pl.loop(skipped, table[START, last])
    def _(i):
        r = table[ORDER, i]
        pltpu.make_async_copy(received.at[i - skipped], blocks.at[r], block_sems.at[r]).start()


def wait_blocks(first, last, table, blocks, block_sems):
    @pl.loop(table[START, first], table[START, last])
    def _(i):
        r = table[ORDER, i]
        pltpu.make_async_copy(blocks.at[r], blocks.at[r], block_sems.at[r]).wait()


def load_kernel(sizes, early, table_in, left, right, *refs):
    *units, lefts, rights, blocks, table, block_sems, sems = refs
    loads = [
        pltpu.make_async_copy(left, lefts, sems.at[0]),
        pltpu.make_async_copy(right, rights, sems.at[1]),
    ]
    for load in loads:
        load.start()
    read_table(table_in, table, sems.at[2])
    fetch_own(grouped(units, sizes[3]), 0, table, blocks, block_sems)
    wait_blocks(0, early, table, blocks, block_sems)
    for load in loads:
        load.wait()


def fill_kernel(sizes, early, table_in, received, *refs):
    chips = sizes[4]
    *units, _, blocks, table, block_sems, sem = refs
    read_table(table_in, table, sem)
    fetch_received(received, chips, chips + early, table, blocks, block_sems)
    fetch_own(grouped(units, sizes[3]), early, table, blocks, block_sems)
    wait_blocks(early, chips + early, table, blocks, block_sems)


def product_kernel(sizes, early, first, count, table_in, received, lefts, rights, _, *refs):
    targets, terms, classes, op_size, chips = sizes
    keep, send, blocks, table, block_sems, sem = refs
    size = lefts.shape[-1]
    rows = size // op_size
    me = lax.axis_index("op")
    read_table(table_in, table, sem)
    if first == 0:
        fetch_received(received, chips + early, 2 * chips, table, blocks, block_sems)
        if count < targets:
            wait_blocks(chips + early, 2 * chips, table, blocks, block_sems)

    @pl.loop(0, count)
    def _(step):
        t = first + step

        if count == targets:

            @pl.loop(0, classes)
            def _(c):
                r = t * classes + c

                @pl.when(table[LATER, r] == 1)
                def _():
                    pltpu.make_async_copy(blocks.at[r], blocks.at[r], block_sems.at[r]).wait()

        lifted = []
        for o in range(terms):
            block = blocks[t * classes + table[CLASS, o]].reshape(size, size)
            lifted.append(
                jnp.dot(lefts[t, o], block, preferred_element_type=jnp.float32).astype(jnp.bfloat16)
            )
        total = lax.dot_general(
            jnp.concatenate(lifted, axis=1),
            jnp.concatenate([rights[t, o] for o in range(terms)], axis=1),
            (((1,), (1,)), ((), ())),
            preferred_element_type=jnp.float32,
        )
        for j in range(op_size):
            part = total[j * rows : (j + 1) * rows]
            distance = lax.rem(j + op_size - me, op_size)

            @pl.when(distance == 0)
            def _():
                keep[step] = part

            @pl.when(distance != 0)
            def _():
                send[distance - 1, step] = part.astype(jnp.bfloat16)


def shards(wave, left_ops, right_ops, owner_map, local_map, op_class):
    chips, op_size = lax.axis_size("chip"), lax.axis_size("op")
    targets, terms, size, _ = left_ops.shape
    sec_dev, rows, _ = wave.shape
    classes = owner_map.shape[1]
    half = chips // 2
    asked = targets * classes
    sizes = (targets, terms, classes, op_size, chips)
    early = chips - 3
    most = max(2, (asked + 2 * chips - 1) // (2 * chips) + 1)
    ring = list(range(0, chips, 2)) + list(range(1, chips, 2))[::-1]

    def hop(x):
        pairs = [
            (2 * ring[i] + core, 2 * ring[(i + 1 - 2 * core) % chips] + core)
            for i in range(chips)
            for core in range(2)
        ]
        return lax.ppermute(x, ("chip", "core"), pairs)

    def swap(x):
        return lax.ppermute(x, "core", [(0, 1), (1, 0)])

    def across(x):
        return [
            lax.ppermute(x, "op", [((q + j) % op_size, q) for q in range(op_size)])
            for j in range(1, op_size)
        ]

    whole = pl.BlockSpec(memory_space=pltpu.VMEM)
    scalars = pl.BlockSpec(memory_space=pltpu.SMEM)
    apart = pl.BlockSpec(memory_space=pl.ANY)
    def call(kernel, name, operands, outs, scratch, specs=None, aliases={}, flops=0):
        return pl.pallas_call(
            kernel,
            name=name,
            in_specs=specs or [whole] + [apart] * (len(operands) - 1),
            out_specs=[whole] * len(outs),
            out_shape=outs,
            input_output_aliases=aliases,
            scratch_shapes=[pltpu.SMEM(TABLE, jnp.int32)] + scratch,
            compiler_params=pltpu.CompilerParams(vmem_limit_bytes=LIMITS[name] * 1024 * 1024),
            cost_estimate=pl.CostEstimate(
                flops=flops, bytes_accessed=sum(2 * x.size for x in outs), transcendentals=0
            ),
        )(*operands)

    (table,) = call(
        functools.partial(table_kernel, sizes, early),
        "table",
        [owner_map, local_map, op_class],
        [jax.ShapeDtypeStruct(TABLE, jnp.int32)],
        [
            pltpu.SMEM((asked,), jnp.int32),
            pltpu.SMEM((2 * chips,), jnp.int32),
            pltpu.SemaphoreType.DMA,
        ],
        [scalars] * 3,
    )

    rules = {'other': [('crossed', -2)]}

    @functools.cache
    def arrived(kind, k):
        if k == 0:
            return dict(own=lambda: [wave], other=lambda: [swap(wave)], beside=lambda: across(wave))[kind]()
        x = arrived("other", k) if kind == "crossed" else arrived(kind, k - 1)
        done = []
        for before, shift in rules.get(kind, ()):
            most_hops = half - 1 if before in ("other", "crossed") else half
            if 1 <= k + shift <= most_hops:
                done += arrived(before, k + shift)
        if done:
            x = [lax.optimization_barrier((y, *done))[0] for y in x]
        if (kind, k) == ('beside', 1):
            x = [lax.optimization_barrier((y, table))[0] for y in x]
        if kind == "crossed":
            return across(x[0])
        return [hop(y) for y in x]

    units = [[wave] + arrived("beside", 0)]
    for k in range(1, half):
        units += [arrived("own", k) + arrived("beside", k), arrived("other", k) + arrived("crossed", k)]
    units.append(arrived("own", half) + arrived("beside", half))

    block_shape = (op_size, rows, size)
    blocks_out = jax.ShapeDtypeStruct((asked,) + block_shape, jnp.bfloat16)
    block_sems = [pltpu.SemaphoreType.DMA((asked,)), pltpu.SemaphoreType.DMA]

    def flat(low, high, ties=()):
        arrays = [x for unit in units[low:high] for x in unit]
        tied = [x for kind, k in ties for x in arrived(kind, k)]
        return arrays[:-1] + [lax.optimization_barrier((arrays[-1], *tied))[0]] if tied else arrays

    their_table = swap(table)
    operators_out = [jax.ShapeDtypeStruct(x.shape, jnp.bfloat16) for x in (left_ops, right_ops)]
    lefts, rights, blocks = call(
        functools.partial(load_kernel, sizes, early),
        "load",
        [table, left_ops, right_ops] + flat(0, early, (('own', 4),)),
        operators_out + [blocks_out],
        [pltpu.SemaphoreType.DMA((asked,)), pltpu.SemaphoreType.DMA((3,))],
    )
    received = []
    for low, high, ties in ((0, early, ()), (early, chips, ())):
        slots = min(asked, (high - low) * most)
        arrays = flat(low, high, ties)
        if low == early and True:
            arrays[0] = lax.optimization_barrier((arrays[0], lefts))[0]
        (sent,) = call(
            functools.partial(sent_kernel, sizes, low, high),
            "sent",
            [their_table] + arrays,
            [jax.ShapeDtypeStruct((slots,) + block_shape, jnp.bfloat16)],
            [pltpu.SemaphoreType.DMA((slots,)), pltpu.SemaphoreType.DMA],
        )
        received.append(swap(sent))
    operands = [table, received[0]] + flat(early, chips) + [blocks]
    (blocks,) = call(
        functools.partial(fill_kernel, sizes, early),
        "fill",
        operands,
        [blocks_out],
        block_sems,
        [whole] + [apart] * (len(operands) - 2) + [whole],
        {len(operands) - 1: 0},
    )

    results = []
    for first in range(0, targets, 6):
        count = min(6, targets - first)
        keep, send, blocks = call(
            functools.partial(product_kernel, sizes, early, first, count),
            "product",
            [table, received[1], lefts, rights, blocks],
            [
                jax.ShapeDtypeStruct((count, rows, size), jnp.float32),
                jax.ShapeDtypeStruct((op_size - 1, count, rows, size), jnp.bfloat16),
                blocks_out,
            ],
            block_sems,
            [whole, apart] + [whole] * 3,
            {4: 2},
            4 * count * terms * size**3,
        )
        for k in range(1, op_size):
            turn = [(p, (p + k) % op_size) for p in range(op_size)]
            keep = keep + lax.ppermute(send[k - 1], "op", turn).astype(jnp.float32)
        results.append(keep.astype(jnp.bfloat16))
    return jnp.concatenate(results)


def solution(mesh):
    sec_size, op_size = mesh.shape["sec"], mesh.shape["op"]
    split = Mesh(mesh.devices.reshape(sec_size // 2, 2, op_size), ("chip", "core", "op"))
    sec = ("chip", "core")
    in_specs = (
        P(sec, "op", None),
        P(sec, "op", None, None),
        P(sec, "op", None, None),
        P(sec, None),
        P(sec, None),
        P("op"),
    )
    out_specs = P(sec, "op", None)
    return jax.shard_map(shards, mesh=split, in_specs=in_specs, out_specs=out_specs, check_vma=False)
```

```python
import functools

import jax
import jax.numpy as jnp
from jax import lax
from jax.experimental import pallas as pl
from jax.experimental.pallas import tpu as pltpu
from jax.sharding import Mesh, PartitionSpec as P

ORDER, START, SECTOR, CLASS, LATER = range(5)
TABLE = (8, 128)
LIMITS = dict(table=4, sent=8, load=32, fill=8, product=24)


def ring_position(chip, chips):
    return jnp.where(lax.rem(chip, 2) == 0, lax.div(chip, 2), chips - 1 - lax.div(chip, 2))


def table_kernel(sizes, early, owner_map, local_map, op_class, *refs):
    targets, terms, classes, op_size, chips = sizes
    half = chips // 2
    core = lax.axis_index("core")
    place = ring_position(lax.axis_index("chip"), chips)
    table_out, table, unit_of, filled, sem = refs

    @pl.loop(0, 2 * chips)
    def _(u):
        filled[u] = 0

    @pl.loop(0, targets)
    def _(t):
        @pl.loop(0, classes)
        def _(c):
            r = t * classes + c
            owner = owner_map[t, c]
            owner_core = owner & 1
            chip = owner >> 1
            position = jnp.where((chip & 1) == 0, chip >> 1, chips - 1 - (chip >> 1))
            offset = position - place
            offset = jnp.where(offset < 0, offset + chips, offset)
            distance = jnp.minimum(offset, chips - offset)
            end = (distance == 0) | (distance == half)
            holder = jnp.where(end, owner_core, jnp.where(offset > half, 0, 1))
            unit = jnp.where(distance == 0, 0, 2 * distance - jnp.where(owner_core == holder, 1, 0))
            away = jnp.where(holder == core, 0, 1)
            slot = unit + away * chips
            unit_of[r] = slot
            filled[slot] = filled[slot] + 1
            table[SECTOR, r] = local_map[t, c]
            table[LATER, r] = jnp.where((away == 1) & (unit >= early), 1, 0)

    for o in range(terms):
        table[CLASS, o] = op_class[o]

    def place_unit(u, at):
        table[START, u] = at
        count = filled[u]
        filled[u] = at
        return at + count

    table[START, 2 * chips] = lax.fori_loop(0, 2 * chips, place_unit, jnp.int32(0))

    @pl.loop(0, targets * classes)
    def _(r):
        u = unit_of[r]
        at = filled[u]
        table[ORDER, at] = r
        filled[u] = at + 1

    out = pltpu.make_async_copy(table, table_out, sem)
    out.start()
    out.wait()


def fetch(unit, sector, target, sem):
    op_size = len(unit)
    me = lax.axis_index("op")
    for j, source in enumerate(unit):
        pltpu.make_async_copy(source.at[sector], target.at[lax.rem(me + j, op_size)], sem).start()


def read_table(source, target, sem):
    copy = pltpu.make_async_copy(source, target, sem)
    copy.start()
    copy.wait()


def grouped(refs, size):
    return [refs[i : i + size] for i in range(0, len(refs), size)]


def sent_kernel(sizes, low, high, asked_in, *refs):
    chips, op_size = sizes[4], sizes[3]
    *units, sent, table, slot_sems, sem = refs
    read_table(asked_in, table, sem)
    skipped = table[START, chips + low]
    for u, unit in enumerate(grouped(units, op_size), low):

        @pl.loop(table[START, chips + u], table[START, chips + u + 1])
        def _(i):
            slot = i - skipped
            fetch(unit, table[SECTOR, table[ORDER, i]], sent.at[slot], slot_sems.at[slot])

    @pl.loop(0, table[START, chips + high] - skipped)
    def _(slot):
        pltpu.make_async_copy(sent.at[slot], sent.at[slot], slot_sems.at[slot]).wait()


def fetch_own(units, low, table, blocks, block_sems):
    for u, unit in enumerate(units, low):

        @pl.loop(table[START, u], table[START, u + 1])
        def _(i):
            r = table[ORDER, i]
            fetch(unit, table[SECTOR, r], blocks.at[r], block_sems.at[r])


def fetch_received(received, first, last, table, blocks, block_sems):
    skipped = table[START, first]

    @pl.loop(skipped, table[START, last])
    def _(i):
        r = table[ORDER, i]
        pltpu.make_async_copy(received.at[i - skipped], blocks.at[r], block_sems.at[r]).start()


def wait_blocks(first, last, table, blocks, block_sems):
    @pl.loop(table[START, first], table[START, last])
    def _(i):
        r = table[ORDER, i]
        pltpu.make_async_copy(blocks.at[r], blocks.at[r], block_sems.at[r]).wait()


def load_kernel(sizes, early, table_in, left, right, *refs):
    *units, lefts, rights, blocks, table, block_sems, sems = refs
    loads = [
        pltpu.make_async_copy(left, lefts, sems.at[0]),
        pltpu.make_async_copy(right, rights, sems.at[1]),
    ]
    for load in loads:
        load.start()
    read_table(table_in, table, sems.at[2])
    fetch_own(grouped(units, sizes[3]), 0, table, blocks, block_sems)
    wait_blocks(0, early, table, blocks, block_sems)
    for load in loads:
        load.wait()


def fill_kernel(sizes, early, table_in, received, *refs):
    chips = sizes[4]
    *units, _, blocks, table, block_sems, sem = refs
    read_table(table_in, table, sem)
    fetch_received(received, chips, chips + early, table, blocks, block_sems)
    fetch_own(grouped(units, sizes[3]), early, table, blocks, block_sems)
    wait_blocks(early, chips + early, table, blocks, block_sems)


def product_kernel(sizes, early, first, count, table_in, received, lefts, rights, _, *refs):
    targets, terms, classes, op_size, chips = sizes
    keep, send, blocks, table, block_sems, sem = refs
    size = lefts.shape[-1]
    rows = size // op_size
    me = lax.axis_index("op")
    read_table(table_in, table, sem)
    if first == 0:
        fetch_received(received, chips + early, 2 * chips, table, blocks, block_sems)
        if count < targets:
            wait_blocks(chips + early, 2 * chips, table, blocks, block_sems)

    @pl.loop(0, count)
    def _(step):
        t = first + step

        if count == targets:

            @pl.loop(0, classes)
            def _(c):
                r = t * classes + c

                @pl.when(table[LATER, r] == 1)
                def _():
                    pltpu.make_async_copy(blocks.at[r], blocks.at[r], block_sems.at[r]).wait()

        lifted = []
        for o in range(terms):
            block = blocks[t * classes + table[CLASS, o]].reshape(size, size)
            lifted.append(
                jnp.dot(lefts[t, o], block, preferred_element_type=jnp.float32).astype(jnp.bfloat16)
            )
        total = lax.dot_general(
            jnp.concatenate(lifted, axis=1),
            jnp.concatenate([rights[t, o] for o in range(terms)], axis=1),
            (((1,), (1,)), ((), ())),
            preferred_element_type=jnp.float32,
        )
        for j in range(op_size):
            part = total[j * rows : (j + 1) * rows]
            distance = lax.rem(j + op_size - me, op_size)

            @pl.when(distance == 0)
            def _():
                keep[step] = part

            @pl.when(distance != 0)
            def _():
                send[distance - 1, step] = part.astype(jnp.bfloat16)


def shards(wave, left_ops, right_ops, owner_map, local_map, op_class):
    chips, op_size = lax.axis_size("chip"), lax.axis_size("op")
    targets, terms, size, _ = left_ops.shape
    sec_dev, rows, _ = wave.shape
    classes = owner_map.shape[1]
    half = chips // 2
    asked = targets * classes
    sizes = (targets, terms, classes, op_size, chips)
    early = chips - 3
    most = max(2, (asked + 2 * chips - 1) // (2 * chips) + 1)
    ring = list(range(0, chips, 2)) + list(range(1, chips, 2))[::-1]

    def hop(x):
        pairs = [
            (2 * ring[i] + core, 2 * ring[(i + 1 - 2 * core) % chips] + core)
            for i in range(chips)
            for core in range(2)
        ]
        return lax.ppermute(x, ("chip", "core"), pairs)

    def swap(x):
        return lax.ppermute(x, "core", [(0, 1), (1, 0)])

    def across(x):
        return [
            lax.ppermute(x, "op", [((q + j) % op_size, q) for q in range(op_size)])
            for j in range(1, op_size)
        ]

    whole = pl.BlockSpec(memory_space=pltpu.VMEM)
    scalars = pl.BlockSpec(memory_space=pltpu.SMEM)
    apart = pl.BlockSpec(memory_space=pl.ANY)
    def call(kernel, name, operands, outs, scratch, specs=None, aliases={}, flops=0):
        return pl.pallas_call(
            kernel,
            name=name,
            in_specs=specs or [whole] + [apart] * (len(operands) - 1),
            out_specs=[whole] * len(outs),
            out_shape=outs,
            input_output_aliases=aliases,
            scratch_shapes=[pltpu.SMEM(TABLE, jnp.int32)] + scratch,
            compiler_params=pltpu.CompilerParams(vmem_limit_bytes=LIMITS[name] * 1024 * 1024),
            cost_estimate=pl.CostEstimate(
                flops=flops, bytes_accessed=sum(2 * x.size for x in outs), transcendentals=0
            ),
        )(*operands)

    (table,) = call(
        functools.partial(table_kernel, sizes, early),
        "table",
        [owner_map, local_map, op_class],
        [jax.ShapeDtypeStruct(TABLE, jnp.int32)],
        [
            pltpu.SMEM((asked,), jnp.int32),
            pltpu.SMEM((2 * chips,), jnp.int32),
            pltpu.SemaphoreType.DMA,
        ],
        [scalars] * 3,
    )

    rules = {'crossed': [('beside', -2)], 'other': [('beside', -2), ('crossed', -2)], 'own': [('other', -1)]}

    @functools.cache
    def arrived(kind, k):
        if k == 0:
            return dict(own=lambda: [wave], other=lambda: [swap(wave)], beside=lambda: across(wave))[kind]()
        x = arrived("other", k) if kind == "crossed" else arrived(kind, k - 1)
        done = []
        for before, shift in rules.get(kind, ()):
            most_hops = half - 1 if before in ("other", "crossed") else half
            if 1 <= k + shift <= most_hops:
                done += arrived(before, k + shift)
        if done:
            x = [lax.optimization_barrier((y, *done))[0] for y in x]
        if (kind, k) == ('beside', 1):
            x = [lax.optimization_barrier((y, table))[0] for y in x]
        if kind == "crossed":
            return across(x[0])
        return [hop(y) for y in x]

    units = [[wave] + arrived("beside", 0)]
    for k in range(1, half):
        units += [arrived("own", k) + arrived("beside", k), arrived("other", k) + arrived("crossed", k)]
    units.append(arrived("own", half) + arrived("beside", half))

    block_shape = (op_size, rows, size)
    blocks_out = jax.ShapeDtypeStruct((asked,) + block_shape, jnp.bfloat16)
    block_sems = [pltpu.SemaphoreType.DMA((asked,)), pltpu.SemaphoreType.DMA]

    def flat(low, high, ties=()):
        arrays = [x for unit in units[low:high] for x in unit]
        tied = [x for kind, k in ties for x in arrived(kind, k)]
        return arrays[:-1] + [lax.optimization_barrier((arrays[-1], *tied))[0]] if tied else arrays

    their_table = swap(table)
    operators_out = [jax.ShapeDtypeStruct(x.shape, jnp.bfloat16) for x in (left_ops, right_ops)]
    lefts, rights, blocks = call(
        functools.partial(load_kernel, sizes, early),
        "load",
        [table, left_ops, right_ops] + flat(0, early, (('own', 4),)),
        operators_out + [blocks_out],
        [pltpu.SemaphoreType.DMA((asked,)), pltpu.SemaphoreType.DMA((3,))],
    )
    received = []
    for low, high, ties in ((0, early, ()), (early, chips, ())):
        slots = min(asked, (high - low) * most)
        arrays = flat(low, high, ties)
        if low == early and True:
            arrays[0] = lax.optimization_barrier((arrays[0], lefts))[0]
        (sent,) = call(
            functools.partial(sent_kernel, sizes, low, high),
            "sent",
            [their_table] + arrays,
            [jax.ShapeDtypeStruct((slots,) + block_shape, jnp.bfloat16)],
            [pltpu.SemaphoreType.DMA((slots,)), pltpu.SemaphoreType.DMA],
        )
        received.append(swap(sent))
    operands = [table, received[0]] + flat(early, chips) + [blocks]
    (blocks,) = call(
        functools.partial(fill_kernel, sizes, early),
        "fill",
        operands,
        [blocks_out],
        block_sems,
        [whole] + [apart] * (len(operands) - 2) + [whole],
        {len(operands) - 1: 0},
    )

    results = []
    for first in range(0, targets, 4):
        count = min(4, targets - first)
        keep, send, blocks = call(
            functools.partial(product_kernel, sizes, early, first, count),
            "product",
            [table, received[1], lefts, rights, blocks],
            [
                jax.ShapeDtypeStruct((count, rows, size), jnp.float32),
                jax.ShapeDtypeStruct((op_size - 1, count, rows, size), jnp.bfloat16),
                blocks_out,
            ],
            block_sems,
            [whole, apart] + [whole] * 3,
            {4: 2},
            4 * count * terms * size**3,
        )
        for k in range(1, op_size):
            turn = [(p, (p + k) % op_size) for p in range(op_size)]
            keep = keep + lax.ppermute(send[k - 1], "op", turn).astype(jnp.float32)
        results.append(keep.astype(jnp.bfloat16))
    return jnp.concatenate(results)


def solution(mesh):
    sec_size, op_size = mesh.shape["sec"], mesh.shape["op"]
    split = Mesh(mesh.devices.reshape(sec_size // 2, 2, op_size), ("chip", "core", "op"))
    sec = ("chip", "core")
    in_specs = (
        P(sec, "op", None),
        P(sec, "op", None, None),
        P(sec, "op", None, None),
        P(sec, None),
        P(sec, None),
        P("op"),
    )
    out_specs = P(sec, "op", None)
    return jax.shard_map(shards, mesh=split, in_specs=in_specs, out_specs=out_specs, check_vma=False)
```

```python
import functools

import jax
import jax.numpy as jnp
from jax import lax
from jax.experimental import pallas as pl
from jax.experimental.pallas import tpu as pltpu
from jax.sharding import Mesh, PartitionSpec as P

ORDER, START, SECTOR, CLASS, LATER = range(5)
TABLE = (8, 128)
LIMITS = dict(table=4, sent=8, load=32, fill=8, product=24)


def ring_position(chip, chips):
    return jnp.where(lax.rem(chip, 2) == 0, lax.div(chip, 2), chips - 1 - lax.div(chip, 2))


def table_kernel(sizes, early, owner_map, local_map, op_class, wave, *refs):
    targets, terms, classes, op_size, chips = sizes
    half = chips // 2
    core = lax.axis_index("core")
    place = ring_position(lax.axis_index("chip"), chips)
    table_out, wave_out, table, unit_of, filled, sems = refs
    wave_copy = pltpu.make_async_copy(wave, wave_out, sems.at[0])
    wave_copy.start()

    @pl.loop(0, 2 * chips)
    def _(u):
        filled[u] = 0

    @pl.loop(0, targets)
    def _(t):
        @pl.loop(0, classes)
        def _(c):
            r = t * classes + c
            owner = owner_map[t, c]
            owner_core = owner & 1
            chip = owner >> 1
            position = jnp.where((chip & 1) == 0, chip >> 1, chips - 1 - (chip >> 1))
            offset = position - place
            offset = jnp.where(offset < 0, offset + chips, offset)
            distance = jnp.minimum(offset, chips - offset)
            end = (distance == 0) | (distance == half)
            holder = jnp.where(end, owner_core, jnp.where(offset > half, 0, 1))
            unit = jnp.where(distance == 0, 0, 2 * distance - jnp.where(owner_core == holder, 1, 0))
            away = jnp.where(holder == core, 0, 1)
            slot = unit + away * chips
            unit_of[r] = slot
            filled[slot] = filled[slot] + 1
            table[SECTOR, r] = local_map[t, c]
            table[LATER, r] = jnp.where((away == 1) & (unit >= early), 1, 0)

    for o in range(terms):
        table[CLASS, o] = op_class[o]

    def place_unit(u, at):
        table[START, u] = at
        count = filled[u]
        filled[u] = at
        return at + count

    table[START, 2 * chips] = lax.fori_loop(0, 2 * chips, place_unit, jnp.int32(0))

    @pl.loop(0, targets * classes)
    def _(r):
        u = unit_of[r]
        at = filled[u]
        table[ORDER, at] = r
        filled[u] = at + 1

    out = pltpu.make_async_copy(table, table_out, sems.at[1])
    out.start()
    out.wait()
    wave_copy.wait()


def fetch(unit, sector, target, sem):
    op_size = len(unit)
    me = lax.axis_index("op")
    for j, source in enumerate(unit):
        pltpu.make_async_copy(source.at[sector], target.at[lax.rem(me + j, op_size)], sem).start()


def read_table(source, target, sem):
    copy = pltpu.make_async_copy(source, target, sem)
    copy.start()
    copy.wait()


def grouped(refs, size):
    return [refs[i : i + size] for i in range(0, len(refs), size)]


def sent_kernel(sizes, low, high, asked_in, *refs):
    chips, op_size = sizes[4], sizes[3]
    *units, sent, table, slot_sems, sem = refs
    read_table(asked_in, table, sem)
    skipped = table[START, chips + low]
    for u, unit in enumerate(grouped(units, op_size), low):

        @pl.loop(table[START, chips + u], table[START, chips + u + 1])
        def _(i):
            slot = i - skipped
            fetch(unit, table[SECTOR, table[ORDER, i]], sent.at[slot], slot_sems.at[slot])

    @pl.loop(0, table[START, chips + high] - skipped)
    def _(slot):
        pltpu.make_async_copy(sent.at[slot], sent.at[slot], slot_sems.at[slot]).wait()


def fetch_own(units, low, table, blocks, block_sems):
    for u, unit in enumerate(units, low):

        @pl.loop(table[START, u], table[START, u + 1])
        def _(i):
            r = table[ORDER, i]
            fetch(unit, table[SECTOR, r], blocks.at[r], block_sems.at[r])


def fetch_received(received, first, last, table, blocks, block_sems):
    skipped = table[START, first]

    @pl.loop(skipped, table[START, last])
    def _(i):
        r = table[ORDER, i]
        pltpu.make_async_copy(received.at[i - skipped], blocks.at[r], block_sems.at[r]).start()


def wait_blocks(first, last, table, blocks, block_sems):
    @pl.loop(table[START, first], table[START, last])
    def _(i):
        r = table[ORDER, i]
        pltpu.make_async_copy(blocks.at[r], blocks.at[r], block_sems.at[r]).wait()


def load_kernel(sizes, early, table_in, left, right, *refs):
    *units, lefts, rights, blocks, table, block_sems, sems = refs
    loads = [
        pltpu.make_async_copy(left, lefts, sems.at[0]),
        pltpu.make_async_copy(right, rights, sems.at[1]),
    ]
    for load in loads:
        load.start()
    read_table(table_in, table, sems.at[2])
    fetch_own(grouped(units, sizes[3]), 0, table, blocks, block_sems)
    wait_blocks(0, early, table, blocks, block_sems)
    for load in loads:
        load.wait()


def fill_kernel(sizes, early, table_in, received, *refs):
    chips = sizes[4]
    *units, _, blocks, table, block_sems, sem = refs
    read_table(table_in, table, sem)
    fetch_received(received, chips, chips + early, table, blocks, block_sems)
    fetch_own(grouped(units, sizes[3]), early, table, blocks, block_sems)
    wait_blocks(early, chips + early, table, blocks, block_sems)


def product_kernel(sizes, early, first, count, table_in, received, lefts, rights, _, *refs):
    targets, terms, classes, op_size, chips = sizes
    keep, send, blocks, table, block_sems, sem = refs
    size = lefts.shape[-1]
    rows = size // op_size
    me = lax.axis_index("op")
    read_table(table_in, table, sem)
    if first == 0:
        fetch_received(received, chips + early, 2 * chips, table, blocks, block_sems)
        if count < targets:
            wait_blocks(chips + early, 2 * chips, table, blocks, block_sems)

    @pl.loop(0, count)
    def _(step):
        t = first + step

        if count == targets:

            @pl.loop(0, classes)
            def _(c):
                r = t * classes + c

                @pl.when(table[LATER, r] == 1)
                def _():
                    pltpu.make_async_copy(blocks.at[r], blocks.at[r], block_sems.at[r]).wait()

        lifted = []
        for o in range(terms):
            block = blocks[t * classes + table[CLASS, o]].reshape(size, size)
            lifted.append(
                jnp.dot(lefts[t, o], block, preferred_element_type=jnp.float32).astype(jnp.bfloat16)
            )
        total = lax.dot_general(
            jnp.concatenate(lifted, axis=1),
            jnp.concatenate([rights[t, o] for o in range(terms)], axis=1),
            (((1,), (1,)), ((), ())),
            preferred_element_type=jnp.float32,
        )
        for j in range(op_size):
            part = total[j * rows : (j + 1) * rows]
            distance = lax.rem(j + op_size - me, op_size)

            @pl.when(distance == 0)
            def _():
                keep[step] = part

            @pl.when(distance != 0)
            def _():
                send[distance - 1, step] = part.astype(jnp.bfloat16)


def held_kernel(source, out):
    del source, out


def shards(wave, left_ops, right_ops, owner_map, local_map, op_class):
    chips, op_size = lax.axis_size("chip"), lax.axis_size("op")
    targets, terms, size, _ = left_ops.shape
    sec_dev, rows, _ = wave.shape
    classes = owner_map.shape[1]
    half = chips // 2
    asked = targets * classes
    sizes = (targets, terms, classes, op_size, chips)
    early = chips - 3
    most = max(2, (asked + 2 * chips - 1) // (2 * chips) + 1)
    ring = list(range(0, chips, 2)) + list(range(1, chips, 2))[::-1]

    def hop(x):
        pairs = [
            (2 * ring[i] + core, 2 * ring[(i + 1 - 2 * core) % chips] + core)
            for i in range(chips)
            for core in range(2)
        ]
        return lax.ppermute(x, ("chip", "core"), pairs)

    def swap(x):
        return lax.ppermute(x, "core", [(0, 1), (1, 0)])

    def across(x):
        return [
            lax.ppermute(x, "op", [((q + j) % op_size, q) for q in range(op_size)])
            for j in range(1, op_size)
        ]

    whole = pl.BlockSpec(memory_space=pltpu.VMEM)
    scalars = pl.BlockSpec(memory_space=pltpu.SMEM)
    apart = pl.BlockSpec(memory_space=pl.ANY)
    def call(kernel, name, operands, outs, scratch, specs=None, aliases={}, flops=0):
        return pl.pallas_call(
            kernel,
            name=name,
            in_specs=specs or [whole] + [apart] * (len(operands) - 1),
            out_specs=[whole] * len(outs),
            out_shape=outs,
            input_output_aliases=aliases,
            scratch_shapes=[pltpu.SMEM(TABLE, jnp.int32)] + scratch,
            compiler_params=pltpu.CompilerParams(vmem_limit_bytes=LIMITS[name] * 1024 * 1024),
            cost_estimate=pl.CostEstimate(
                flops=flops, bytes_accessed=sum(2 * x.size for x in outs), transcendentals=0
            ),
        )(*operands)

    table, wave_near = call(
        functools.partial(table_kernel, sizes, early),
        "table",
        [owner_map, local_map, op_class, wave],
        [jax.ShapeDtypeStruct(TABLE, jnp.int32), jax.ShapeDtypeStruct(wave.shape, wave.dtype)],
        [
            pltpu.SMEM((asked,), jnp.int32),
            pltpu.SMEM((2 * chips,), jnp.int32),
            pltpu.SemaphoreType.DMA((2,)),
        ],
        [scalars] * 3 + [apart],
    )

    rules = {'other': [('crossed', -2)]}

    @functools.cache
    def arrived(kind, k):
        if k == 0:
            return dict(own=lambda: [wave], other=lambda: [swap(wave)], beside=lambda: across(wave))[kind]()
        x = arrived("other", k) if kind == "crossed" else arrived(kind, k - 1)
        done = []
        for before, shift in (*rules.get(kind, ()), *rules.get((kind, k), ())):
            most_hops = half - 1 if before in ("other", "crossed") else half
            if 1 <= k + shift <= most_hops:
                done += arrived(before, k + shift)
        if done:
            x = [lax.optimization_barrier((y, *done))[0] for y in x]
        if (kind, k) == ('beside', 1):
            x = [lax.optimization_barrier((y, table))[0] for y in x]
        if kind == "crossed":
            return across(x[0])
        return [hop(y) for y in x]

    units = [[wave_near] + arrived("beside", 0)]
    for k in range(1, half):
        units += [arrived("own", k) + arrived("beside", k), arrived("other", k) + arrived("crossed", k)]
    units.append(arrived("own", half) + arrived("beside", half))

    block_shape = (op_size, rows, size)
    blocks_out = jax.ShapeDtypeStruct((asked,) + block_shape, jnp.bfloat16)
    block_sems = [pltpu.SemaphoreType.DMA((asked,)), pltpu.SemaphoreType.DMA]

    def flat(low, high, ties=()):
        arrays = [x for unit in units[low:high] for x in unit]
        tied = [x for kind, k in ties for x in arrived(kind, k)]
        return arrays[:-1] + [lax.optimization_barrier((arrays[-1], *tied))[0]] if tied else arrays

    their_table = swap(table)

    def gather(low, high, arrays):
        slots = min(asked, (high - low) * most)
        (sent,) = call(
            functools.partial(sent_kernel, sizes, low, high),
            "sent",
            [their_table] + arrays,
            [jax.ShapeDtypeStruct((slots,) + block_shape, jnp.bfloat16)],
            [pltpu.SemaphoreType.DMA((slots,)), pltpu.SemaphoreType.DMA],
        )
        return swap(sent)

    first_received = gather(0, early, flat(0, early, ()))
    operators_out = [jax.ShapeDtypeStruct(x.shape, jnp.bfloat16) for x in (left_ops, right_ops)]
    lefts, rights, blocks = call(
        functools.partial(load_kernel, sizes, early),
        "load",
        [table, left_ops, right_ops] + flat(0, early, (('own', 4),)),
        operators_out + [blocks_out],
        [pltpu.SemaphoreType.DMA((asked,)), pltpu.SemaphoreType.DMA((3,))],
    )
    late = flat(early, chips)
    received = gather(early, chips, [lax.optimization_barrier((late[0], lefts))[0]] + late[1:])
    operands = [table, first_received] + late + [blocks]
    (blocks,) = call(
        functools.partial(fill_kernel, sizes, early),
        "fill",
        operands,
        [blocks_out],
        block_sems,
        [whole] + [apart] * (len(late) + 1) + [whole],
        {len(operands) - 1: 0},
    )

    results, held = [], []
    parts = [targets - 2, 2]
    for first, count in zip([sum(parts[:i]) for i in range(len(parts))], parts):
        keep, send, blocks = call(
            functools.partial(product_kernel, sizes, early, first, count),
            "product",
            [table, received, lefts, rights, blocks],
            [
                jax.ShapeDtypeStruct((count, rows, size), jnp.float32),
                jax.ShapeDtypeStruct((op_size - 1, count, rows, size), jnp.bfloat16),
                blocks_out,
            ],
            block_sems,
            [whole, apart] + [whole] * 3,
            {4: 2},
            4 * count * terms * size**3,
        )
        for k in range(1, op_size):
            turn = [(p, (p + k) % op_size) for p in range(op_size)]
            part = lax.ppermute(send[k - 1], "op", turn)
            if first + count < targets:
                part = pl.pallas_call(
                    held_kernel,
                    name="held",
                    in_specs=[apart],
                    out_specs=apart,
                    out_shape=jax.ShapeDtypeStruct(part.shape, part.dtype),
                    input_output_aliases={0: 0},
                    cost_estimate=pl.CostEstimate(
                        flops=0, bytes_accessed=100 * part.size, transcendentals=0
                    ),
                )(part)
                held.append(part)
            elif held:
                keep = lax.optimization_barrier((keep, *held))[0]
            keep = keep + part.astype(jnp.float32)
        results.append(keep.astype(jnp.bfloat16))
    return jnp.concatenate(results)


def solution(mesh):
    sec_size, op_size = mesh.shape["sec"], mesh.shape["op"]
    split = Mesh(mesh.devices.reshape(sec_size // 2, 2, op_size), ("chip", "core", "op"))
    sec = ("chip", "core")
    in_specs = (
        P(sec, "op", None),
        P(sec, "op", None, None),
        P(sec, "op", None, None),
        P(sec, None),
        P(sec, None),
        P("op"),
    )
    out_specs = P(sec, "op", None)
    return jax.shard_map(shards, mesh=split, in_specs=in_specs, out_specs=out_specs, check_vma=False)
```

```python
import functools

import jax
import jax.numpy as jnp
from jax import lax
from jax.experimental import pallas as pl
from jax.experimental.pallas import tpu as pltpu
from jax.sharding import Mesh, PartitionSpec as P

ORDER, START, SECTOR, CLASS, LATER = range(5)
TABLE = (8, 128)
LIMITS = dict(table=4, sent=8, load=32, fill=8, product=24)


def ring_position(chip, chips):
    return jnp.where(lax.rem(chip, 2) == 0, lax.div(chip, 2), chips - 1 - lax.div(chip, 2))


def table_kernel(sizes, early, owner_map, local_map, op_class, wave, *refs):
    targets, terms, classes, op_size, chips = sizes
    half = chips // 2
    core = lax.axis_index("core")
    place = ring_position(lax.axis_index("chip"), chips)
    table_out, wave_out, table, unit_of, filled, sems = refs
    wave_copy = pltpu.make_async_copy(wave, wave_out, sems.at[0])
    wave_copy.start()

    @pl.loop(0, 2 * chips)
    def _(u):
        filled[u] = 0

    @pl.loop(0, targets)
    def _(t):
        @pl.loop(0, classes)
        def _(c):
            r = t * classes + c
            owner = owner_map[t, c]
            owner_core = owner & 1
            chip = owner >> 1
            position = jnp.where((chip & 1) == 0, chip >> 1, chips - 1 - (chip >> 1))
            offset = position - place
            offset = jnp.where(offset < 0, offset + chips, offset)
            distance = jnp.minimum(offset, chips - offset)
            end = (distance == 0) | (distance == half)
            holder = jnp.where(end, owner_core, jnp.where(offset > half, 0, 1))
            unit = jnp.where(distance == 0, 0, 2 * distance - jnp.where(owner_core == holder, 1, 0))
            away = jnp.where(holder == core, 0, 1)
            slot = unit + away * chips
            unit_of[r] = slot
            filled[slot] = filled[slot] + 1
            table[SECTOR, r] = local_map[t, c]
            table[LATER, r] = jnp.where((away == 1) & (unit >= early), 1, 0)

    for o in range(terms):
        table[CLASS, o] = op_class[o]

    def place_unit(u, at):
        table[START, u] = at
        count = filled[u]
        filled[u] = at
        return at + count

    table[START, 2 * chips] = lax.fori_loop(0, 2 * chips, place_unit, jnp.int32(0))

    @pl.loop(0, targets * classes)
    def _(r):
        u = unit_of[r]
        at = filled[u]
        table[ORDER, at] = r
        filled[u] = at + 1

    out = pltpu.make_async_copy(table, table_out, sems.at[1])
    out.start()
    out.wait()
    wave_copy.wait()


def fetch(unit, sector, target, sem):
    op_size = len(unit)
    me = lax.axis_index("op")
    for j, source in enumerate(unit):
        pltpu.make_async_copy(source.at[sector], target.at[lax.rem(me + j, op_size)], sem).start()


def read_table(source, target, sem):
    copy = pltpu.make_async_copy(source, target, sem)
    copy.start()
    copy.wait()


def grouped(refs, size):
    return [refs[i : i + size] for i in range(0, len(refs), size)]


def sent_kernel(sizes, low, high, asked_in, *refs):
    chips, op_size = sizes[4], sizes[3]
    *units, sent, table, slot_sems, sem = refs
    read_table(asked_in, table, sem)
    skipped = table[START, chips + low]
    for u, unit in enumerate(grouped(units, op_size), low):

        @pl.loop(table[START, chips + u], table[START, chips + u + 1])
        def _(i):
            slot = i - skipped
            fetch(unit, table[SECTOR, table[ORDER, i]], sent.at[slot], slot_sems.at[slot])

    @pl.loop(0, table[START, chips + high] - skipped)
    def _(slot):
        pltpu.make_async_copy(sent.at[slot], sent.at[slot], slot_sems.at[slot]).wait()


def fetch_own(units, low, table, blocks, block_sems):
    for u, unit in enumerate(units, low):

        @pl.loop(table[START, u], table[START, u + 1])
        def _(i):
            r = table[ORDER, i]
            fetch(unit, table[SECTOR, r], blocks.at[r], block_sems.at[r])


def fetch_received(received, first, last, table, blocks, block_sems):
    skipped = table[START, first]

    @pl.loop(skipped, table[START, last])
    def _(i):
        r = table[ORDER, i]
        pltpu.make_async_copy(received.at[i - skipped], blocks.at[r], block_sems.at[r]).start()


def wait_blocks(first, last, table, blocks, block_sems):
    @pl.loop(table[START, first], table[START, last])
    def _(i):
        r = table[ORDER, i]
        pltpu.make_async_copy(blocks.at[r], blocks.at[r], block_sems.at[r]).wait()


def load_kernel(sizes, early, table_in, left, right, *refs):
    *units, lefts, rights, blocks, table, block_sems, sems = refs
    loads = [
        pltpu.make_async_copy(left, lefts, sems.at[0]),
        pltpu.make_async_copy(right, rights, sems.at[1]),
    ]
    for load in loads:
        load.start()
    read_table(table_in, table, sems.at[2])
    fetch_own(grouped(units, sizes[3]), 0, table, blocks, block_sems)
    wait_blocks(0, early, table, blocks, block_sems)
    for load in loads:
        load.wait()


def fill_kernel(sizes, early, table_in, received, *refs):
    chips = sizes[4]
    *units, _, blocks, table, block_sems, sem = refs
    read_table(table_in, table, sem)
    fetch_received(received, chips, chips + early, table, blocks, block_sems)
    fetch_own(grouped(units, sizes[3]), early, table, blocks, block_sems)
    wait_blocks(early, chips + early, table, blocks, block_sems)


def product_kernel(sizes, early, first, count, table_in, received, lefts, rights, _, *refs):
    targets, terms, classes, op_size, chips = sizes
    keep, send, blocks, table, block_sems, sem = refs
    size = lefts.shape[-1]
    rows = size // op_size
    me = lax.axis_index("op")
    read_table(table_in, table, sem)
    if first == 0:
        fetch_received(received, chips + early, 2 * chips, table, blocks, block_sems)
        if count < targets:
            wait_blocks(chips + early, 2 * chips, table, blocks, block_sems)

    @pl.loop(0, count)
    def _(step):
        t = first + step

        if count == targets:

            @pl.loop(0, classes)
            def _(c):
                r = t * classes + c

                @pl.when(table[LATER, r] == 1)
                def _():
                    pltpu.make_async_copy(blocks.at[r], blocks.at[r], block_sems.at[r]).wait()

        lifted = []
        for o in range(terms):
            block = blocks[t * classes + table[CLASS, o]].reshape(size, size)
            lifted.append(
                jnp.dot(lefts[t, o], block, preferred_element_type=jnp.float32).astype(jnp.bfloat16)
            )
        total = lax.dot_general(
            jnp.concatenate(lifted, axis=1),
            jnp.concatenate([rights[t, o] for o in range(terms)], axis=1),
            (((1,), (1,)), ((), ())),
            preferred_element_type=jnp.float32,
        )
        for j in range(op_size):
            part = total[j * rows : (j + 1) * rows]
            distance = lax.rem(j + op_size - me, op_size)

            @pl.when(distance == 0)
            def _():
                keep[step] = part

            @pl.when(distance != 0)
            def _():
                send[distance - 1, step] = part.astype(jnp.bfloat16)


def held_kernel(source, out):
    del source, out


def shards(wave, left_ops, right_ops, owner_map, local_map, op_class):
    chips, op_size = lax.axis_size("chip"), lax.axis_size("op")
    targets, terms, size, _ = left_ops.shape
    sec_dev, rows, _ = wave.shape
    classes = owner_map.shape[1]
    half = chips // 2
    asked = targets * classes
    sizes = (targets, terms, classes, op_size, chips)
    early = chips - 3
    most = max(2, (asked + 2 * chips - 1) // (2 * chips) + 1)
    ring = list(range(0, chips, 2)) + list(range(1, chips, 2))[::-1]

    def hop(x):
        pairs = [
            (2 * ring[i] + core, 2 * ring[(i + 1 - 2 * core) % chips] + core)
            for i in range(chips)
            for core in range(2)
        ]
        return lax.ppermute(x, ("chip", "core"), pairs)

    def swap(x):
        return lax.ppermute(x, "core", [(0, 1), (1, 0)])

    def across(x):
        return [
            lax.ppermute(x, "op", [((q + j) % op_size, q) for q in range(op_size)])
            for j in range(1, op_size)
        ]

    whole = pl.BlockSpec(memory_space=pltpu.VMEM)
    scalars = pl.BlockSpec(memory_space=pltpu.SMEM)
    apart = pl.BlockSpec(memory_space=pl.ANY)
    def call(kernel, name, operands, outs, scratch, specs=None, aliases={}, flops=0):
        return pl.pallas_call(
            kernel,
            name=name,
            in_specs=specs or [whole] + [apart] * (len(operands) - 1),
            out_specs=[whole] * len(outs),
            out_shape=outs,
            input_output_aliases=aliases,
            scratch_shapes=[pltpu.SMEM(TABLE, jnp.int32)] + scratch,
            compiler_params=pltpu.CompilerParams(vmem_limit_bytes=LIMITS[name] * 1024 * 1024),
            cost_estimate=pl.CostEstimate(
                flops=flops, bytes_accessed=sum(2 * x.size for x in outs), transcendentals=0
            ),
        )(*operands)

    table, wave_near = call(
        functools.partial(table_kernel, sizes, early),
        "table",
        [owner_map, local_map, op_class, wave],
        [jax.ShapeDtypeStruct(TABLE, jnp.int32), jax.ShapeDtypeStruct(wave.shape, wave.dtype)],
        [
            pltpu.SMEM((asked,), jnp.int32),
            pltpu.SMEM((2 * chips,), jnp.int32),
            pltpu.SemaphoreType.DMA((2,)),
        ],
        [scalars] * 3 + [apart],
    )

    rules = {'other': [('crossed', -2)], ('crossed', 2): [('beside', -1)], ('own', 3): [('beside', -1)]}

    @functools.cache
    def arrived(kind, k):
        if k == 0:
            return dict(own=lambda: [wave], other=lambda: [swap(wave)], beside=lambda: across(wave))[kind]()
        x = arrived("other", k) if kind == "crossed" else arrived(kind, k - 1)
        done = []
        for before, shift in (*rules.get(kind, ()), *rules.get((kind, k), ())):
            most_hops = half - 1 if before in ("other", "crossed") else half
            if 1 <= k + shift <= most_hops:
                done += arrived(before, k + shift)
        if done:
            x = [lax.optimization_barrier((y, *done))[0] for y in x]
        if (kind, k) == ('beside', 1):
            x = [lax.optimization_barrier((y, table))[0] for y in x]
        if kind == "crossed":
            return across(x[0])
        return [hop(y) for y in x]

    units = [[wave_near] + arrived("beside", 0)]
    for k in range(1, half):
        units += [arrived("own", k) + arrived("beside", k), arrived("other", k) + arrived("crossed", k)]
    units.append(arrived("own", half) + arrived("beside", half))

    block_shape = (op_size, rows, size)
    blocks_out = jax.ShapeDtypeStruct((asked,) + block_shape, jnp.bfloat16)
    block_sems = [pltpu.SemaphoreType.DMA((asked,)), pltpu.SemaphoreType.DMA]

    def flat(low, high, ties=()):
        arrays = [x for unit in units[low:high] for x in unit]
        tied = [x for kind, k in ties for x in arrived(kind, k)]
        return arrays[:-1] + [lax.optimization_barrier((arrays[-1], *tied))[0]] if tied else arrays

    their_table = swap(table)

    def gather(low, high, arrays):
        slots = min(asked, (high - low) * most)
        (sent,) = call(
            functools.partial(sent_kernel, sizes, low, high),
            "sent",
            [their_table] + arrays,
            [jax.ShapeDtypeStruct((slots,) + block_shape, jnp.bfloat16)],
            [pltpu.SemaphoreType.DMA((slots,)), pltpu.SemaphoreType.DMA],
        )
        return swap(sent)

    first_received = gather(0, early, flat(0, early, (('crossed', 2),)))
    operators_out = [jax.ShapeDtypeStruct(x.shape, jnp.bfloat16) for x in (left_ops, right_ops)]
    lefts, rights, blocks = call(
        functools.partial(load_kernel, sizes, early),
        "load",
        [table, left_ops, right_ops] + flat(0, early, ()),
        operators_out + [blocks_out],
        [pltpu.SemaphoreType.DMA((asked,)), pltpu.SemaphoreType.DMA((3,))],
    )
    late = flat(early, chips)
    received = gather(early, chips, [lax.optimization_barrier((late[0], lefts))[0]] + late[1:])
    operands = [table, first_received] + late + [blocks]
    (blocks,) = call(
        functools.partial(fill_kernel, sizes, early),
        "fill",
        operands,
        [blocks_out],
        block_sems,
        [whole] + [apart] * (len(late) + 1) + [whole],
        {len(operands) - 1: 0},
    )

    results, held = [], []
    parts = [targets - 2, 2]
    for first, count in zip([sum(parts[:i]) for i in range(len(parts))], parts):
        keep, send, blocks = call(
            functools.partial(product_kernel, sizes, early, first, count),
            "product",
            [table, received, lefts, rights, blocks],
            [
                jax.ShapeDtypeStruct((count, rows, size), jnp.float32),
                jax.ShapeDtypeStruct((op_size - 1, count, rows, size), jnp.bfloat16),
                blocks_out,
            ],
            block_sems,
            [whole, apart] + [whole] * 3,
            {4: 2},
            4 * count * terms * size**3,
        )
        for k in range(1, op_size):
            turn = [(p, (p + k) % op_size) for p in range(op_size)]
            part = lax.ppermute(send[k - 1], "op", turn)
            if first + count < targets:
                part = pl.pallas_call(
                    held_kernel,
                    name="held",
                    in_specs=[apart],
                    out_specs=apart,
                    out_shape=jax.ShapeDtypeStruct(part.shape, part.dtype),
                    input_output_aliases={0: 0},
                    cost_estimate=pl.CostEstimate(
                        flops=0, bytes_accessed=100 * part.size, transcendentals=0
                    ),
                )(part)
                held.append(part)
            elif held:
                keep = lax.optimization_barrier((keep, *held))[0]
            keep = keep + part.astype(jnp.float32)
        results.append(keep.astype(jnp.bfloat16))
    return jnp.concatenate(results)


def solution(mesh):
    sec_size, op_size = mesh.shape["sec"], mesh.shape["op"]
    split = Mesh(mesh.devices.reshape(sec_size // 2, 2, op_size), ("chip", "core", "op"))
    sec = ("chip", "core")
    in_specs = (
        P(sec, "op", None),
        P(sec, "op", None, None),
        P(sec, "op", None, None),
        P(sec, None),
        P(sec, None),
        P("op"),
    )
    out_specs = P(sec, "op", None)
    return jax.shard_map(shards, mesh=split, in_specs=in_specs, out_specs=out_specs, check_vma=False)
```

```python
import functools

import jax
import jax.numpy as jnp
from jax import lax
from jax.experimental import pallas as pl
from jax.experimental.pallas import tpu as pltpu
from jax.sharding import Mesh, PartitionSpec as P

ORDER, START, SECTOR, CLASS, LATER = range(5)
TABLE = (8, 128)
LIMITS = dict(table=4, sent=8, load=30, fill=8, product=24)


def ring_position(chip, chips):
    return jnp.where(lax.rem(chip, 2) == 0, lax.div(chip, 2), chips - 1 - lax.div(chip, 2))


def table_kernel(sizes, early, owner_map, local_map, op_class, wave, *refs):
    targets, terms, classes, op_size, chips = sizes
    half = chips // 2
    core = lax.axis_index("core")
    place = ring_position(lax.axis_index("chip"), chips)
    table_out, wave_out, table, unit_of, filled, sems = refs
    wave_copy = pltpu.make_async_copy(wave, wave_out, sems.at[0])
    wave_copy.start()

    @pl.loop(0, 2 * chips)
    def _(u):
        filled[u] = 0

    @pl.loop(0, targets)
    def _(t):
        @pl.loop(0, classes)
        def _(c):
            r = t * classes + c
            owner = owner_map[t, c]
            owner_core = owner & 1
            chip = owner >> 1
            position = jnp.where((chip & 1) == 0, chip >> 1, chips - 1 - (chip >> 1))
            offset = position - place
            offset = jnp.where(offset < 0, offset + chips, offset)
            distance = jnp.minimum(offset, chips - offset)
            end = (distance == 0) | (distance == half)
            holder = jnp.where(end, owner_core, jnp.where(offset > half, 0, 1))
            unit = jnp.where(distance == 0, 0, 2 * distance - jnp.where(owner_core == holder, 1, 0))
            away = jnp.where(holder == core, 0, 1)
            slot = unit + away * chips
            unit_of[r] = slot
            filled[slot] = filled[slot] + 1
            table[SECTOR, r] = local_map[t, c]
            table[LATER, r] = jnp.where((away == 1) & (unit >= early), 1, 0)

    for o in range(terms):
        table[CLASS, o] = op_class[o]

    def place_unit(u, at):
        table[START, u] = at
        count = filled[u]
        filled[u] = at
        return at + count

    table[START, 2 * chips] = lax.fori_loop(0, 2 * chips, place_unit, jnp.int32(0))

    @pl.loop(0, targets * classes)
    def _(r):
        u = unit_of[r]
        at = filled[u]
        table[ORDER, at] = r
        filled[u] = at + 1

    out = pltpu.make_async_copy(table, table_out, sems.at[1])
    out.start()
    out.wait()
    wave_copy.wait()


def fetch(unit, sector, target, sem):
    op_size = len(unit)
    me = lax.axis_index("op")
    for j, source in enumerate(unit):
        pltpu.make_async_copy(source.at[sector], target.at[lax.rem(me + j, op_size)], sem).start()


def read_table(source, target, sem):
    copy = pltpu.make_async_copy(source, target, sem)
    copy.start()
    copy.wait()


def grouped(refs, size):
    return [refs[i : i + size] for i in range(0, len(refs), size)]


def sent_kernel(sizes, low, high, asked_in, *refs):
    chips, op_size = sizes[4], sizes[3]
    *units, sent, table, slot_sems, sem = refs
    read_table(asked_in, table, sem)
    skipped = table[START, chips + low]
    for u, unit in enumerate(grouped(units, op_size), low):

        @pl.loop(table[START, chips + u], table[START, chips + u + 1])
        def _(i):
            slot = i - skipped
            fetch(unit, table[SECTOR, table[ORDER, i]], sent.at[slot], slot_sems.at[slot])

    @pl.loop(0, table[START, chips + high] - skipped)
    def _(slot):
        pltpu.make_async_copy(sent.at[slot], sent.at[slot], slot_sems.at[slot]).wait()


def fetch_own(units, low, table, blocks, block_sems):
    for u, unit in enumerate(units, low):

        @pl.loop(table[START, u], table[START, u + 1])
        def _(i):
            r = table[ORDER, i]
            fetch(unit, table[SECTOR, r], blocks.at[r], block_sems.at[r])


def fetch_received(received, first, last, table, blocks, block_sems):
    skipped = table[START, first]

    @pl.loop(skipped, table[START, last])
    def _(i):
        r = table[ORDER, i]
        pltpu.make_async_copy(received.at[i - skipped], blocks.at[r], block_sems.at[r]).start()


def wait_blocks(first, last, table, blocks, block_sems):
    @pl.loop(table[START, first], table[START, last])
    def _(i):
        r = table[ORDER, i]
        pltpu.make_async_copy(blocks.at[r], blocks.at[r], block_sems.at[r]).wait()


def load_kernel(sizes, early, table_in, left, right, *refs):
    targets, terms = sizes[0], sizes[1]
    *units, lefts, turned, blocks, table, rights, block_sems, right_sems, sems = refs
    size = lefts.shape[-1]
    loads = [
        pltpu.make_async_copy(right.at[t], rights.at[t], right_sems.at[t]) for t in range(targets)
    ]
    left_load = pltpu.make_async_copy(left, lefts, sems.at[0])
    for load in loads + [left_load]:
        load.start()
    read_table(table_in, table, sems.at[1])
    fetch_own(grouped(units, sizes[3]), 0, table, blocks, block_sems)
    for t in range(targets):
        loads[t].wait()
        for o in range(terms):
            turned[t, o * size : (o + 1) * size] = rights[t, o].T
    wait_blocks(0, early, table, blocks, block_sems)
    left_load.wait()


def fill_kernel(sizes, early, table_in, received, *refs):
    chips = sizes[4]
    *units, _, blocks, table, block_sems, sem = refs
    read_table(table_in, table, sem)
    fetch_received(received, chips, chips + early, table, blocks, block_sems)
    fetch_own(grouped(units, sizes[3]), early + 1, table, blocks, block_sems)
    wait_blocks(early + 1, chips + early, table, blocks, block_sems)


def product_kernel(sizes, early, first, count, table_in, received, lefts, rights, _, *refs):
    targets, terms, classes, op_size, chips = sizes
    keep, send, blocks, table, block_sems, sem = refs
    size = lefts.shape[-1]
    rows = size // op_size
    me = lax.axis_index("op")
    read_table(table_in, table, sem)
    if first == 0:
        fetch_received(received, chips + early, 2 * chips, table, blocks, block_sems)
        if count < targets:
            wait_blocks(chips + early, 2 * chips, table, blocks, block_sems)

    @pl.loop(0, count)
    def _(step):
        t = first + step

        if count == targets:

            @pl.loop(0, classes)
            def _(c):
                r = t * classes + c

                @pl.when(table[LATER, r] == 1)
                def _():
                    pltpu.make_async_copy(blocks.at[r], blocks.at[r], block_sems.at[r]).wait()

        lifted = []
        for o in range(terms):
            block = blocks[t * classes + table[CLASS, o]].reshape(size, size)
            lifted.append(
                jnp.dot(lefts[t, o], block, preferred_element_type=jnp.float32).astype(jnp.bfloat16)
            )
        total = lax.dot_general(
            jnp.concatenate(lifted, axis=1),
            rights[t],
            (((1,), (0,)), ((), ())),
            preferred_element_type=jnp.float32,
        )
        for j in range(op_size):
            part = total[j * rows : (j + 1) * rows]
            distance = lax.rem(j + op_size - me, op_size)

            @pl.when(distance == 0)
            def _():
                keep[step] = part

            @pl.when(distance != 0)
            def _():
                send[distance - 1, step] = part.astype(jnp.bfloat16)


def held_kernel(source, out):
    del source, out


def shards(wave, left_ops, right_ops, owner_map, local_map, op_class):
    chips, op_size = lax.axis_size("chip"), lax.axis_size("op")
    targets, terms, size, _ = left_ops.shape
    sec_dev, rows, _ = wave.shape
    classes = owner_map.shape[1]
    half = chips // 2
    asked = targets * classes
    sizes = (targets, terms, classes, op_size, chips)
    early = chips - 3
    most = max(2, (asked + 2 * chips - 1) // (2 * chips) + 1)
    ring = list(range(0, chips, 2)) + list(range(1, chips, 2))[::-1]

    def hop(x):
        pairs = [
            (2 * ring[i] + core, 2 * ring[(i + 1 - 2 * core) % chips] + core)
            for i in range(chips)
            for core in range(2)
        ]
        return lax.ppermute(x, ("chip", "core"), pairs)

    def swap(x):
        return lax.ppermute(x, "core", [(0, 1), (1, 0)])

    def across(x):
        return [
            lax.ppermute(x, "op", [((q + j) % op_size, q) for q in range(op_size)])
            for j in range(1, op_size)
        ]

    whole = pl.BlockSpec(memory_space=pltpu.VMEM)
    scalars = pl.BlockSpec(memory_space=pltpu.SMEM)
    apart = pl.BlockSpec(memory_space=pl.ANY)
    def call(kernel, name, operands, outs, scratch, specs=None, aliases={}, flops=0):
        return pl.pallas_call(
            kernel,
            name=name,
            in_specs=specs or [whole] + [apart] * (len(operands) - 1),
            out_specs=[whole] * len(outs),
            out_shape=outs,
            input_output_aliases=aliases,
            scratch_shapes=[pltpu.SMEM(TABLE, jnp.int32)] + scratch,
            compiler_params=pltpu.CompilerParams(vmem_limit_bytes=LIMITS[name] * 1024 * 1024),
            cost_estimate=pl.CostEstimate(
                flops=flops, bytes_accessed=sum(2 * x.size for x in outs), transcendentals=0
            ),
        )(*operands)

    table, wave_near = call(
        functools.partial(table_kernel, sizes, early),
        "table",
        [owner_map, local_map, op_class, wave],
        [jax.ShapeDtypeStruct(TABLE, jnp.int32), jax.ShapeDtypeStruct(wave.shape, wave.dtype)],
        [
            pltpu.SMEM((asked,), jnp.int32),
            pltpu.SMEM((2 * chips,), jnp.int32),
            pltpu.SemaphoreType.DMA((2,)),
        ],
        [scalars] * 3 + [apart],
    )

    rules = {'other': [('crossed', -2)], ('crossed', 2): [('beside', -1)], ('own', 3): [('beside', -1)]}

    @functools.cache
    def arrived(kind, k):
        if k == 0:
            return dict(own=lambda: [wave], other=lambda: [swap(wave)], beside=lambda: across(wave))[kind]()
        x = arrived("other", k) if kind == "crossed" else arrived(kind, k - 1)
        done = []
        for before, shift in (*rules.get(kind, ()), *rules.get((kind, k), ())):
            most_hops = half - 1 if before in ("other", "crossed") else half
            if 1 <= k + shift <= most_hops:
                done += arrived(before, k + shift)
        if done:
            x = [lax.optimization_barrier((y, *done))[0] for y in x]
        if (kind, k) == ('beside', 1):
            x = [lax.optimization_barrier((y, table))[0] for y in x]
        if kind == "crossed":
            return across(x[0])
        return [hop(y) for y in x]

    units = [[wave_near] + arrived("beside", 0)]
    for k in range(1, half):
        units += [arrived("own", k) + arrived("beside", k), arrived("other", k) + arrived("crossed", k)]
    units.append(arrived("own", half) + arrived("beside", half))

    block_shape = (op_size, rows, size)
    blocks_out = jax.ShapeDtypeStruct((asked,) + block_shape, jnp.bfloat16)
    block_sems = [pltpu.SemaphoreType.DMA((asked,)), pltpu.SemaphoreType.DMA]

    def flat(low, high, ties=()):
        arrays = [x for unit in units[low:high] for x in unit]
        tied = [x for kind, k in ties for x in arrived(kind, k)]
        return arrays[:-1] + [lax.optimization_barrier((arrays[-1], *tied))[0]] if tied else arrays

    their_table = swap(table)

    def gather(low, high, arrays):
        slots = min(asked, (high - low) * most)
        (sent,) = call(
            functools.partial(sent_kernel, sizes, low, high),
            "sent",
            [their_table] + arrays,
            [jax.ShapeDtypeStruct((slots,) + block_shape, jnp.bfloat16)],
            [pltpu.SemaphoreType.DMA((slots,)), pltpu.SemaphoreType.DMA],
        )
        return swap(sent)

    first_received = gather(0, early, flat(0, early, (('crossed', 2),)))
    operators_out = [
        jax.ShapeDtypeStruct(left_ops.shape, jnp.bfloat16),
        jax.ShapeDtypeStruct((targets, terms * size, size), jnp.bfloat16),
    ]
    lefts, rights, blocks = call(
        functools.partial(load_kernel, sizes, early + 1),
        "load",
        [table, left_ops, right_ops] + flat(0, early + 1, ()),
        operators_out + [blocks_out],
        [
            pltpu.VMEM(right_ops.shape, jnp.bfloat16),
            pltpu.SemaphoreType.DMA((asked,)),
            pltpu.SemaphoreType.DMA((targets,)),
            pltpu.SemaphoreType.DMA((2,)),
        ],
    )
    late = flat(early, chips)
    received = gather(early, chips, [lax.optimization_barrier((late[0], lefts))[0]] + late[1:])
    last = flat(early + 1, chips)
    operands = [table, first_received] + last + [blocks]
    (blocks,) = call(
        functools.partial(fill_kernel, sizes, early),
        "fill",
        operands,
        [blocks_out],
        block_sems,
        [whole] + [apart] * (len(last) + 1) + [whole],
        {len(operands) - 1: 0},
    )

    results, held = [], []
    parts = [targets - 2, 2]
    for first, count in zip([sum(parts[:i]) for i in range(len(parts))], parts):
        keep, send, blocks = call(
            functools.partial(product_kernel, sizes, early, first, count),
            "product",
            [table, received, lefts, rights, blocks],
            [
                jax.ShapeDtypeStruct((count, rows, size), jnp.float32),
                jax.ShapeDtypeStruct((op_size - 1, count, rows, size), jnp.bfloat16),
                blocks_out,
            ],
            block_sems,
            [whole, apart] + [whole] * 3,
            {4: 2},
            4 * count * terms * size**3,
        )
        for k in range(1, op_size):
            turn = [(p, (p + k) % op_size) for p in range(op_size)]
            part = lax.ppermute(send[k - 1], "op", turn)
            if first + count < targets:
                part = pl.pallas_call(
                    held_kernel,
                    name="held",
                    in_specs=[apart],
                    out_specs=apart,
                    out_shape=jax.ShapeDtypeStruct(part.shape, part.dtype),
                    input_output_aliases={0: 0},
                    cost_estimate=pl.CostEstimate(
                        flops=0, bytes_accessed=100 * part.size, transcendentals=0
                    ),
                )(part)
                held.append(part)
            elif held:
                keep = lax.optimization_barrier((keep, *held))[0]
            keep = keep + part.astype(jnp.float32)
        results.append(keep.astype(jnp.bfloat16))
    return jnp.concatenate(results)


def solution(mesh):
    sec_size, op_size = mesh.shape["sec"], mesh.shape["op"]
    split = Mesh(mesh.devices.reshape(sec_size // 2, 2, op_size), ("chip", "core", "op"))
    sec = ("chip", "core")
    in_specs = (
        P(sec, "op", None),
        P(sec, "op", None, None),
        P(sec, "op", None, None),
        P(sec, None),
        P(sec, None),
        P("op"),
    )
    out_specs = P(sec, "op", None)
    return jax.shard_map(shards, mesh=split, in_specs=in_specs, out_specs=out_specs, check_vma=False)
```

```python
import functools

import jax
import jax.numpy as jnp
from jax import lax
from jax.experimental import pallas as pl
from jax.experimental.pallas import tpu as pltpu
from jax.sharding import Mesh, PartitionSpec as P

ORDER, START, SECTOR, CLASS, LATER = range(5)
TABLE = (8, 128)
LIMITS = dict(table=4, sent=12, load=32, fill=16, product=28)


def ring_position(chip, chips):
    return jnp.where(lax.rem(chip, 2) == 0, lax.div(chip, 2), chips - 1 - lax.div(chip, 2))


def table_kernel(sizes, early, owner_map, local_map, op_class, wave, *refs):
    targets, terms, classes, op_size, chips, _ = sizes
    half = chips // 2
    core = lax.axis_index("core")
    place = ring_position(lax.axis_index("chip"), chips)
    table_out, wave_out, table, unit_of, filled, sems = refs
    wave_copy = pltpu.make_async_copy(wave, wave_out, sems.at[0])
    wave_copy.start()

    @pl.loop(0, 2 * chips)
    def _(u):
        filled[u] = 0

    @pl.loop(0, targets)
    def _(t):
        @pl.loop(0, classes)
        def _(c):
            r = t * classes + c
            owner = owner_map[t, c]
            owner_core = owner & 1
            chip = owner >> 1
            position = jnp.where((chip & 1) == 0, chip >> 1, chips - 1 - (chip >> 1))
            offset = position - place
            offset = jnp.where(offset < 0, offset + chips, offset)
            distance = jnp.minimum(offset, chips - offset)
            end = (distance == 0) | (distance == half)
            holder = jnp.where(end, owner_core, jnp.where(offset > half, 0, 1))
            unit = jnp.where(distance == 0, 0, 2 * distance - jnp.where(owner_core == holder, 1, 0))
            away = jnp.where(holder == core, 0, 1)
            slot = unit + away * chips
            unit_of[r] = slot
            filled[slot] = filled[slot] + 1
            table[SECTOR, r] = local_map[t, c]
            table[LATER, r] = jnp.where((away == 1) & (unit >= early), 1, 0)

    for o in range(terms):
        table[CLASS, o] = op_class[o]

    def place_unit(u, at):
        table[START, u] = at
        count = filled[u]
        filled[u] = at
        return at + count

    table[START, 2 * chips] = lax.fori_loop(0, 2 * chips, place_unit, jnp.int32(0))

    @pl.loop(0, targets * classes)
    def _(r):
        u = unit_of[r]
        at = filled[u]
        table[ORDER, at] = r
        filled[u] = at + 1

    out = pltpu.make_async_copy(table, table_out, sems.at[1])
    out.start()
    out.wait()
    wave_copy.wait()


def fetch(near, unit, sector, target, r, sem):
    op_size = len(unit)
    me = lax.axis_index("op")
    for j, source in enumerate(unit):
        turn = lax.rem(me + j, op_size)
        if near:
            target[r, turn] = source[sector]
        else:
            pltpu.make_async_copy(source.at[sector], target.at[r, turn], sem).start()


def read_table(source, target, sem):
    copy = pltpu.make_async_copy(source, target, sem)
    copy.start()
    copy.wait()


def grouped(refs, size):
    return [refs[i : i + size] for i in range(0, len(refs), size)]


def sent_kernel(sizes, low, high, asked_in, *refs):
    op_size, chips, near = sizes[3:]
    *units, sent, table, slot_sems, sem = refs
    read_table(asked_in, table, sem)
    skipped = table[START, chips + low]
    for u, unit in enumerate(grouped(units, op_size), low):

        @pl.loop(table[START, chips + u], table[START, chips + u + 1])
        def _(i):
            slot = i - skipped
            fetch(near, unit, table[SECTOR, table[ORDER, i]], sent, slot, slot_sems.at[slot])

    if near:
        return

    @pl.loop(0, table[START, chips + high] - skipped)
    def _(slot):
        pltpu.make_async_copy(sent.at[slot], sent.at[slot], slot_sems.at[slot]).wait()


def fetch_own(near, units, low, table, blocks, block_sems):
    for u, unit in enumerate(units, low):

        @pl.loop(table[START, u], table[START, u + 1])
        def _(i):
            r = table[ORDER, i]
            fetch(near, unit, table[SECTOR, r], blocks, r, block_sems.at[r])


def fetch_received(near, received, first, last, table, blocks, block_sems):
    skipped = table[START, first]

    @pl.loop(skipped, table[START, last])
    def _(i):
        r = table[ORDER, i]
        if near:
            blocks[r] = received[i - skipped]
        else:
            pltpu.make_async_copy(received.at[i - skipped], blocks.at[r], block_sems.at[r]).start()


def wait_blocks(near, first, last, table, blocks, block_sems):
    if near:
        return

    @pl.loop(table[START, first], table[START, last])
    def _(i):
        r = table[ORDER, i]
        pltpu.make_async_copy(blocks.at[r], blocks.at[r], block_sems.at[r]).wait()


def load_kernel(sizes, early, table_in, left, right, *refs):
    *units, lefts, rights, blocks, table, block_sems, sems = refs
    loads = [
        pltpu.make_async_copy(left, lefts, sems.at[0]),
        pltpu.make_async_copy(right, rights, sems.at[1]),
    ]
    for load in loads:
        load.start()
    read_table(table_in, table, sems.at[2])
    fetch_own(sizes[5], grouped(units, sizes[3]), 0, table, blocks, block_sems)
    wait_blocks(sizes[5], 0, early, table, blocks, block_sems)
    for load in loads:
        load.wait()


def fill_kernel(sizes, early, table_in, received, *refs):
    chips = sizes[4]
    *units, _, blocks, table, block_sems, sem = refs
    read_table(table_in, table, sem)
    fetch_received(sizes[5], received, chips, chips + early, table, blocks, block_sems)
    fetch_own(sizes[5], grouped(units, sizes[3]), early, table, blocks, block_sems)
    wait_blocks(sizes[5], early, chips + early, table, blocks, block_sems)


def product_kernel(sizes, early, first, count, table_in, received, lefts, rights, _, *refs):
    targets, terms, classes, op_size, chips, near = sizes
    keep, send, blocks, table, block_sems, sem = refs
    size = lefts.shape[-1]
    rows = size // op_size
    me = lax.axis_index("op")
    read_table(table_in, table, sem)
    if first == 0:
        fetch_received(near, received, chips + early, 2 * chips, table, blocks, block_sems)
        if count < targets:
            wait_blocks(near, chips + early, 2 * chips, table, blocks, block_sems)

    @pl.loop(0, count)
    def _(step):
        t = first + step

        if count == targets and not near:

            @pl.loop(0, classes)
            def _(c):
                r = t * classes + c

                @pl.when(table[LATER, r] == 1)
                def _():
                    pltpu.make_async_copy(blocks.at[r], blocks.at[r], block_sems.at[r]).wait()

        lifted = []
        for o in range(terms):
            block = blocks[t * classes + table[CLASS, o]].reshape(size, size)
            lifted.append(
                jnp.dot(lefts[t, o], block, preferred_element_type=jnp.float32).astype(jnp.bfloat16)
            )
        total = lax.dot_general(
            jnp.concatenate(lifted, axis=1),
            jnp.concatenate([rights[t, o] for o in range(terms)], axis=1),
            (((1,), (1,)), ((), ())),
            preferred_element_type=jnp.float32,
        )
        for j in range(op_size):
            part = total[j * rows : (j + 1) * rows]
            distance = lax.rem(j + op_size - me, op_size)

            @pl.when(distance == 0)
            def _():
                keep[step] = part

            @pl.when(distance != 0)
            def _():
                send[distance - 1, step] = part.astype(jnp.bfloat16)


def held_kernel(source, out):
    del source, out


def shards(wave, left_ops, right_ops, owner_map, local_map, op_class):
    chips, op_size = lax.axis_size("chip"), lax.axis_size("op")
    targets, terms, size, _ = left_ops.shape
    sec_dev, rows, _ = wave.shape
    classes = owner_map.shape[1]
    half = chips // 2
    asked = targets * classes
    near = chips * op_size * wave.size <= 4 * 1024 * 1024
    sizes = (targets, terms, classes, op_size, chips, near)
    early = chips - 3
    most = max(2, (asked + 2 * chips - 1) // (2 * chips) + 1)
    ring = list(range(0, chips, 2)) + list(range(1, chips, 2))[::-1]

    def hop(x):
        pairs = [
            (2 * ring[i] + core, 2 * ring[(i + 1 - 2 * core) % chips] + core)
            for i in range(chips)
            for core in range(2)
        ]
        return lax.ppermute(x, ("chip", "core"), pairs)

    def swap(x):
        return lax.ppermute(x, "core", [(0, 1), (1, 0)])

    def across(x):
        return [
            lax.ppermute(x, "op", [((q + j) % op_size, q) for q in range(op_size)])
            for j in range(1, op_size)
        ]

    whole = pl.BlockSpec(memory_space=pltpu.VMEM)
    scalars = pl.BlockSpec(memory_space=pltpu.SMEM)
    apart = pl.BlockSpec(memory_space=pl.ANY)
    held_in = whole if near else apart
    def call(kernel, name, operands, outs, scratch, specs=None, aliases={}, flops=0):
        return pl.pallas_call(
            kernel,
            name=name,
            in_specs=specs or [whole] + [held_in] * (len(operands) - 1),
            out_specs=[whole] * len(outs),
            out_shape=outs,
            input_output_aliases=aliases,
            scratch_shapes=[pltpu.SMEM(TABLE, jnp.int32)] + scratch,
            compiler_params=pltpu.CompilerParams(vmem_limit_bytes=LIMITS[name] * 1024 * 1024),
            cost_estimate=pl.CostEstimate(
                flops=flops, bytes_accessed=sum(2 * x.size for x in outs), transcendentals=0
            ),
        )(*operands)

    table, wave_near = call(
        functools.partial(table_kernel, sizes, early),
        "table",
        [owner_map, local_map, op_class, wave],
        [jax.ShapeDtypeStruct(TABLE, jnp.int32), jax.ShapeDtypeStruct(wave.shape, wave.dtype)],
        [
            pltpu.SMEM((asked,), jnp.int32),
            pltpu.SMEM((2 * chips,), jnp.int32),
            pltpu.SemaphoreType.DMA((2,)),
        ],
        [scalars] * 3 + [apart],
    )

    rules = {'other': [('crossed', -2)], ('crossed', 2): [('beside', -1)], ('own', 3): [('beside', -1)]}

    @functools.cache
    def arrived(kind, k):
        if k == 0:
            return dict(own=lambda: [wave], other=lambda: [swap(wave)], beside=lambda: across(wave))[kind]()
        x = arrived("other", k) if kind == "crossed" else arrived(kind, k - 1)
        done = []
        for before, shift in (*rules.get(kind, ()), *rules.get((kind, k), ())):
            most_hops = half - 1 if before in ("other", "crossed") else half
            if 1 <= k + shift <= most_hops:
                done += arrived(before, k + shift)
        if done:
            x = [lax.optimization_barrier((y, *done))[0] for y in x]
        if (kind, k) == ('beside', 1):
            x = [lax.optimization_barrier((y, table))[0] for y in x]
        if kind == "crossed":
            return across(x[0])
        return [hop(y) for y in x]

    units = [[wave_near] + arrived("beside", 0)]
    for k in range(1, half):
        units += [arrived("own", k) + arrived("beside", k), arrived("other", k) + arrived("crossed", k)]
    units.append(arrived("own", half) + arrived("beside", half))

    block_shape = (op_size, rows, size)
    blocks_out = jax.ShapeDtypeStruct((asked,) + block_shape, jnp.bfloat16)
    block_sems = [pltpu.SemaphoreType.DMA((asked,)), pltpu.SemaphoreType.DMA]

    def flat(low, high, ties=()):
        arrays = [x for unit in units[low:high] for x in unit]
        tied = [x for kind, k in ties for x in arrived(kind, k)]
        return arrays[:-1] + [lax.optimization_barrier((arrays[-1], *tied))[0]] if tied else arrays

    their_table = swap(table)

    def gather(low, high, arrays):
        slots = min(asked, (high - low) * most)
        (sent,) = call(
            functools.partial(sent_kernel, sizes, low, high),
            "sent",
            [their_table] + arrays,
            [jax.ShapeDtypeStruct((slots,) + block_shape, jnp.bfloat16)],
            [pltpu.SemaphoreType.DMA((slots,)), pltpu.SemaphoreType.DMA],
        )
        return swap(sent)

    first_received = gather(0, early, flat(0, early, (('crossed', 2),)))
    operators_out = [jax.ShapeDtypeStruct(x.shape, jnp.bfloat16) for x in (left_ops, right_ops)]
    lefts, rights, blocks = call(
        functools.partial(load_kernel, sizes, early),
        "load",
        [table, left_ops, right_ops] + flat(0, early, ()),
        operators_out + [blocks_out],
        [pltpu.SemaphoreType.DMA((asked,)), pltpu.SemaphoreType.DMA((3,))],
        [whole] + [apart] * 2 + [held_in] * (early * op_size),
    )
    late = flat(early, chips)
    received = gather(early, chips, [lax.optimization_barrier((late[0], lefts))[0]] + late[1:])
    operands = [table, first_received] + late + [blocks]
    (blocks,) = call(
        functools.partial(fill_kernel, sizes, early),
        "fill",
        operands,
        [blocks_out],
        block_sems,
        [whole] + [held_in] * (len(late) + 1) + [whole],
        {len(operands) - 1: 0},
    )

    results, held = [], []
    parts = [targets - 2, 2]
    for first, count in zip([sum(parts[:i]) for i in range(len(parts))], parts):
        keep, send, blocks = call(
            functools.partial(product_kernel, sizes, early, first, count),
            "product",
            [table, received, lefts, rights, blocks],
            [
                jax.ShapeDtypeStruct((count, rows, size), jnp.float32),
                jax.ShapeDtypeStruct((op_size - 1, count, rows, size), jnp.bfloat16),
                blocks_out,
            ],
            block_sems,
            [whole, held_in] + [whole] * 3,
            {4: 2},
            4 * count * terms * size**3,
        )
        for k in range(1, op_size):
            turn = [(p, (p + k) % op_size) for p in range(op_size)]
            part = lax.ppermute(send[k - 1], "op", turn)
            if first + count < targets:
                part = pl.pallas_call(
                    held_kernel,
                    name="held",
                    in_specs=[apart],
                    out_specs=apart,
                    out_shape=jax.ShapeDtypeStruct(part.shape, part.dtype),
                    input_output_aliases={0: 0},
                    cost_estimate=pl.CostEstimate(
                        flops=0, bytes_accessed=100 * part.size, transcendentals=0
                    ),
                )(part)
                held.append(part)
            elif held:
                keep = lax.optimization_barrier((keep, *held))[0]
            keep = keep + part.astype(jnp.float32)
        results.append(keep.astype(jnp.bfloat16))
    return jnp.concatenate(results)


def solution(mesh):
    sec_size, op_size = mesh.shape["sec"], mesh.shape["op"]
    split = Mesh(mesh.devices.reshape(sec_size // 2, 2, op_size), ("chip", "core", "op"))
    sec = ("chip", "core")
    in_specs = (
        P(sec, "op", None),
        P(sec, "op", None, None),
        P(sec, "op", None, None),
        P(sec, None),
        P(sec, None),
        P("op"),
    )
    out_specs = P(sec, "op", None)
    return jax.shard_map(shards, mesh=split, in_specs=in_specs, out_specs=out_specs, check_vma=False)
```

```python
import functools

import jax
import jax.numpy as jnp
from jax import lax
from jax.experimental import pallas as pl
from jax.experimental.pallas import tpu as pltpu
from jax.sharding import Mesh, PartitionSpec as P

ORDER, START, SECTOR, CLASS, LATER = range(5)
TABLE = (8, 128)
LIMITS = dict(table=4, sent=12, load=32, fill=16, product=28)


def ring_position(chip, chips):
    return jnp.where(lax.rem(chip, 2) == 0, lax.div(chip, 2), chips - 1 - lax.div(chip, 2))


def table_kernel(sizes, early, owner_map, local_map, op_class, wave, *refs):
    targets, terms, classes, op_size, chips, _ = sizes
    half = chips // 2
    core = lax.axis_index("core")
    place = ring_position(lax.axis_index("chip"), chips)
    table_out, wave_out, table, unit_of, filled, sems = refs
    wave_copy = pltpu.make_async_copy(wave, wave_out, sems.at[0])
    wave_copy.start()

    @pl.loop(0, 2 * chips)
    def _(u):
        filled[u] = 0

    @pl.loop(0, targets)
    def _(t):
        @pl.loop(0, classes)
        def _(c):
            r = t * classes + c
            owner = owner_map[t, c]
            owner_core = owner & 1
            chip = owner >> 1
            position = jnp.where((chip & 1) == 0, chip >> 1, chips - 1 - (chip >> 1))
            offset = position - place
            offset = jnp.where(offset < 0, offset + chips, offset)
            distance = jnp.minimum(offset, chips - offset)
            end = (distance == 0) | (distance == half)
            holder = jnp.where(end, owner_core, jnp.where(offset > half, 0, 1))
            unit = jnp.where(distance == 0, 0, 2 * distance - jnp.where(owner_core == holder, 1, 0))
            away = jnp.where(holder == core, 0, 1)
            slot = unit + away * chips
            unit_of[r] = slot
            filled[slot] = filled[slot] + 1
            table[SECTOR, r] = local_map[t, c]
            table[LATER, r] = jnp.where((away == 1) & (unit >= early), 1, 0)

    for o in range(terms):
        table[CLASS, o] = op_class[o]

    def place_unit(u, at):
        table[START, u] = at
        count = filled[u]
        filled[u] = at
        return at + count

    table[START, 2 * chips] = lax.fori_loop(0, 2 * chips, place_unit, jnp.int32(0))

    @pl.loop(0, targets * classes)
    def _(r):
        u = unit_of[r]
        at = filled[u]
        table[ORDER, at] = r
        filled[u] = at + 1

    out = pltpu.make_async_copy(table, table_out, sems.at[1])
    out.start()
    out.wait()
    wave_copy.wait()


def fetch(near, unit, sector, target, r, sem):
    op_size = len(unit)
    me = lax.axis_index("op")
    for j, source in enumerate(unit):
        turn = lax.rem(me + j, op_size)
        if near:
            target[r, turn] = source[sector]
        else:
            pltpu.make_async_copy(source.at[sector], target.at[r, turn], sem).start()


def read_table(source, target, sem):
    copy = pltpu.make_async_copy(source, target, sem)
    copy.start()
    copy.wait()


def grouped(refs, size):
    return [refs[i : i + size] for i in range(0, len(refs), size)]


def sent_kernel(sizes, low, high, asked_in, *refs):
    op_size, chips, near = sizes[3:]
    *units, sent, table, slot_sems, sem = refs
    read_table(asked_in, table, sem)
    skipped = table[START, chips + low]
    for u, unit in enumerate(grouped(units, op_size), low):

        @pl.loop(table[START, chips + u], table[START, chips + u + 1])
        def _(i):
            slot = i - skipped
            fetch(near, unit, table[SECTOR, table[ORDER, i]], sent, slot, slot_sems.at[slot])

    if near:
        return

    @pl.loop(0, table[START, chips + high] - skipped)
    def _(slot):
        pltpu.make_async_copy(sent.at[slot], sent.at[slot], slot_sems.at[slot]).wait()


def fetch_own(near, units, low, table, blocks, block_sems):
    for u, unit in enumerate(units, low):

        @pl.loop(table[START, u], table[START, u + 1])
        def _(i):
            r = table[ORDER, i]
            fetch(near, unit, table[SECTOR, r], blocks, r, block_sems.at[r])


def fetch_received(near, received, first, last, table, blocks, block_sems):
    skipped = table[START, first]

    @pl.loop(skipped, table[START, last])
    def _(i):
        r = table[ORDER, i]
        if near:
            blocks[r] = received[i - skipped]
        else:
            pltpu.make_async_copy(received.at[i - skipped], blocks.at[r], block_sems.at[r]).start()


def wait_blocks(near, first, last, table, blocks, block_sems):
    if near:
        return

    @pl.loop(table[START, first], table[START, last])
    def _(i):
        r = table[ORDER, i]
        pltpu.make_async_copy(blocks.at[r], blocks.at[r], block_sems.at[r]).wait()


def load_kernel(sizes, early, table_in, left, right, *refs):
    *units, lefts, rights, blocks, table, block_sems, sems = refs
    loads = [
        pltpu.make_async_copy(left, lefts, sems.at[0]),
        pltpu.make_async_copy(right, rights, sems.at[1]),
    ]
    for load in loads:
        load.start()
    read_table(table_in, table, sems.at[2])
    fetch_own(sizes[5], grouped(units, sizes[3]), 0, table, blocks, block_sems)
    wait_blocks(sizes[5], 0, early, table, blocks, block_sems)
    for load in loads:
        load.wait()


def fill_kernel(sizes, early, table_in, received, *refs):
    chips = sizes[4]
    *units, _, blocks, table, block_sems, sem = refs
    read_table(table_in, table, sem)
    fetch_received(sizes[5], received, chips, chips + early, table, blocks, block_sems)
    fetch_own(sizes[5], grouped(units, sizes[3]), early, table, blocks, block_sems)
    wait_blocks(sizes[5], early, chips + early, table, blocks, block_sems)


def product_kernel(sizes, early, first, count, table_in, received, lefts, rights, _, *refs):
    targets, terms, classes, op_size, chips, near = sizes
    keep, send, blocks, table, block_sems, sem = refs
    size = lefts.shape[-1]
    rows = size // op_size
    me = lax.axis_index("op")
    read_table(table_in, table, sem)
    if first == 0:
        fetch_received(near, received, chips + early, 2 * chips, table, blocks, block_sems)
        if count < targets:
            wait_blocks(near, chips + early, 2 * chips, table, blocks, block_sems)

    @pl.loop(0, count)
    def _(step):
        t = first + step

        if count == targets and not near:

            @pl.loop(0, classes)
            def _(c):
                r = t * classes + c

                @pl.when(table[LATER, r] == 1)
                def _():
                    pltpu.make_async_copy(blocks.at[r], blocks.at[r], block_sems.at[r]).wait()

        lifted = []
        for o in range(terms):
            block = blocks[t * classes + table[CLASS, o]].reshape(size, size)
            lifted.append(
                jnp.dot(lefts[t, o], block, preferred_element_type=jnp.float32).astype(jnp.bfloat16)
            )
        total = lax.dot_general(
            jnp.concatenate(lifted, axis=1),
            jnp.concatenate([rights[t, o] for o in range(terms)], axis=1),
            (((1,), (1,)), ((), ())),
            preferred_element_type=jnp.float32,
        )
        for j in range(op_size):
            part = total[j * rows : (j + 1) * rows]
            distance = lax.rem(j + op_size - me, op_size)

            @pl.when(distance == 0)
            def _():
                keep[step] = part

            @pl.when(distance != 0)
            def _():
                send[distance - 1, step] = part.astype(jnp.bfloat16)


def held_kernel(source, out):
    del source, out


def shards(wave, left_ops, right_ops, owner_map, local_map, op_class):
    chips, op_size = lax.axis_size("chip"), lax.axis_size("op")
    targets, terms, size, _ = left_ops.shape
    sec_dev, rows, _ = wave.shape
    classes = owner_map.shape[1]
    half = chips // 2
    asked = targets * classes
    near = chips * op_size * wave.size <= 4 * 1024 * 1024
    sizes = (targets, terms, classes, op_size, chips, near)
    early = chips - 3
    most = max(2, (asked + 2 * chips - 1) // (2 * chips) + 1)
    ring = list(range(0, chips, 2)) + list(range(1, chips, 2))[::-1]

    def hop(x):
        pairs = [
            (2 * ring[i] + core, 2 * ring[(i + 1 - 2 * core) % chips] + core)
            for i in range(chips)
            for core in range(2)
        ]
        return lax.ppermute(x, ("chip", "core"), pairs)

    def swap(x):
        return lax.ppermute(x, "core", [(0, 1), (1, 0)])

    def across(x):
        return [
            lax.ppermute(x, "op", [((q + j) % op_size, q) for q in range(op_size)])
            for j in range(1, op_size)
        ]

    whole = pl.BlockSpec(memory_space=pltpu.VMEM)
    scalars = pl.BlockSpec(memory_space=pltpu.SMEM)
    apart = pl.BlockSpec(memory_space=pl.ANY)
    held_in = whole if near else apart
    def call(kernel, name, operands, outs, scratch, specs=None, aliases={}, flops=0):
        return pl.pallas_call(
            kernel,
            name=name,
            in_specs=specs or [whole] + [held_in] * (len(operands) - 1),
            out_specs=[whole] * len(outs),
            out_shape=outs,
            input_output_aliases=aliases,
            scratch_shapes=[pltpu.SMEM(TABLE, jnp.int32)] + scratch,
            compiler_params=pltpu.CompilerParams(vmem_limit_bytes=LIMITS[name] * 1024 * 1024),
            cost_estimate=pl.CostEstimate(
                flops=flops, bytes_accessed=sum(2 * x.size for x in outs), transcendentals=0
            ),
        )(*operands)

    table, wave_near = call(
        functools.partial(table_kernel, sizes, early),
        "table",
        [owner_map, local_map, op_class, wave],
        [jax.ShapeDtypeStruct(TABLE, jnp.int32), jax.ShapeDtypeStruct(wave.shape, wave.dtype)],
        [
            pltpu.SMEM((asked,), jnp.int32),
            pltpu.SMEM((2 * chips,), jnp.int32),
            pltpu.SemaphoreType.DMA((2,)),
        ],
        [scalars] * 3 + [apart],
    )

    rules = {'other': [('crossed', -2)], ('crossed', 2): [('beside', -1)], ('own', 3): [('beside', -1)]}

    @functools.cache
    def arrived(kind, k):
        if k == 0:
            return dict(own=lambda: [wave], other=lambda: [swap(wave)], beside=lambda: across(wave))[kind]()
        x = arrived("other", k) if kind == "crossed" else arrived(kind, k - 1)
        done = []
        for before, shift in (*rules.get(kind, ()), *rules.get((kind, k), ())):
            most_hops = half - 1 if before in ("other", "crossed") else half
            if 1 <= k + shift <= most_hops:
                done += arrived(before, k + shift)
        if done:
            x = [lax.optimization_barrier((y, *done))[0] for y in x]
        if (kind, k) == ('beside', 1):
            x = [lax.optimization_barrier((y, table))[0] for y in x]
        if kind == "crossed":
            return across(x[0])
        return [hop(y) for y in x]

    units = [[wave_near] + arrived("beside", 0)]
    for k in range(1, half):
        units += [arrived("own", k) + arrived("beside", k), arrived("other", k) + arrived("crossed", k)]
    units.append(arrived("own", half) + arrived("beside", half))

    block_shape = (op_size, rows, size)
    blocks_out = jax.ShapeDtypeStruct((asked,) + block_shape, jnp.bfloat16)
    block_sems = [pltpu.SemaphoreType.DMA((asked,)), pltpu.SemaphoreType.DMA]

    def flat(low, high, ties=()):
        arrays = [x for unit in units[low:high] for x in unit]
        tied = [x for kind, k in ties for x in arrived(kind, k)]
        return arrays[:-1] + [lax.optimization_barrier((arrays[-1], *tied))[0]] if tied else arrays

    their_table = swap(table)

    def gather(low, high, arrays):
        slots = min(asked, (high - low) * most)
        (sent,) = call(
            functools.partial(sent_kernel, sizes, low, high),
            "sent",
            [their_table] + arrays,
            [jax.ShapeDtypeStruct((slots,) + block_shape, jnp.bfloat16)],
            [pltpu.SemaphoreType.DMA((slots,)), pltpu.SemaphoreType.DMA],
        )
        return swap(sent)

    first_received = gather(0, early, flat(0, early, (('crossed', 2),)))
    operators_out = [jax.ShapeDtypeStruct(x.shape, jnp.bfloat16) for x in (left_ops, right_ops)]
    lefts, rights, blocks = call(
        functools.partial(load_kernel, sizes, early),
        "load",
        [table, left_ops, right_ops] + flat(0, early, ()),
        operators_out + [blocks_out],
        [pltpu.SemaphoreType.DMA((asked,)), pltpu.SemaphoreType.DMA((3,))],
        [whole] + [apart] * 2 + [held_in] * (early * op_size),
    )
    late = flat(early, chips)
    received = gather(early, chips, [lax.optimization_barrier((late[0], lefts))[0]] + late[1:])
    operands = [table, first_received] + late + [blocks]
    (blocks,) = call(
        functools.partial(fill_kernel, sizes, early),
        "fill",
        operands,
        [blocks_out],
        block_sems,
        [whole] + [held_in] * (len(late) + 1) + [whole],
        {len(operands) - 1: 0},
    )

    results, held = [], []
    parts = [targets - 4, 2, 2]
    for first, count in zip([sum(parts[:i]) for i in range(len(parts))], parts):
        keep, send, blocks = call(
            functools.partial(product_kernel, sizes, early, first, count),
            "product",
            [table, received, lefts, rights, blocks],
            [
                jax.ShapeDtypeStruct((count, rows, size), jnp.float32),
                jax.ShapeDtypeStruct((op_size - 1, count, rows, size), jnp.bfloat16),
                blocks_out,
            ],
            block_sems,
            [whole, held_in] + [whole] * 3,
            {4: 2},
            4 * count * terms * size**3,
        )
        for k in range(1, op_size):
            turn = [(p, (p + k) % op_size) for p in range(op_size)]
            part = lax.ppermute(send[k - 1], "op", turn)
            if first + count < targets:
                part = pl.pallas_call(
                    held_kernel,
                    name="held",
                    in_specs=[apart],
                    out_specs=apart,
                    out_shape=jax.ShapeDtypeStruct(part.shape, part.dtype),
                    input_output_aliases={0: 0},
                    cost_estimate=pl.CostEstimate(
                        flops=0, bytes_accessed=100 * part.size, transcendentals=0
                    ),
                )(part)
                held.append(part)
            elif held:
                keep = lax.optimization_barrier((keep, *held))[0]
            keep = keep + part.astype(jnp.float32)
        results.append(keep.astype(jnp.bfloat16))
    return jnp.concatenate(results)


def solution(mesh):
    sec_size, op_size = mesh.shape["sec"], mesh.shape["op"]
    split = Mesh(mesh.devices.reshape(sec_size // 2, 2, op_size), ("chip", "core", "op"))
    sec = ("chip", "core")
    in_specs = (
        P(sec, "op", None),
        P(sec, "op", None, None),
        P(sec, "op", None, None),
        P(sec, None),
        P(sec, None),
        P("op"),
    )
    out_specs = P(sec, "op", None)
    return jax.shard_map(shards, mesh=split, in_specs=in_specs, out_specs=out_specs, check_vma=False)
```

```python
import functools

import jax
import jax.numpy as jnp
from jax import lax
from jax.experimental import pallas as pl
from jax.experimental.pallas import tpu as pltpu
from jax.sharding import Mesh, PartitionSpec as P

ORDER, START, SECTOR, CLASS, LATER = range(5)
TABLE = (8, 128)
LIMITS = dict(table=4, sent=12, load=32, fill=16, product=28)


def ring_position(chip, chips):
    return jnp.where(lax.rem(chip, 2) == 0, lax.div(chip, 2), chips - 1 - lax.div(chip, 2))


def table_kernel(sizes, early, owner_map, local_map, op_class, wave, *refs):
    targets, terms, classes, op_size, chips, _ = sizes
    half = chips // 2
    core = lax.axis_index("core")
    place = ring_position(lax.axis_index("chip"), chips)
    table_out, wave_out, table, unit_of, filled, sems = refs
    wave_copy = pltpu.make_async_copy(wave, wave_out, sems.at[0])
    wave_copy.start()

    @pl.loop(0, 2 * chips)
    def _(u):
        filled[u] = 0

    @pl.loop(0, targets)
    def _(t):
        @pl.loop(0, classes)
        def _(c):
            r = t * classes + c
            owner = owner_map[t, c]
            owner_core = owner & 1
            chip = owner >> 1
            position = jnp.where((chip & 1) == 0, chip >> 1, chips - 1 - (chip >> 1))
            offset = position - place
            offset = jnp.where(offset < 0, offset + chips, offset)
            distance = jnp.minimum(offset, chips - offset)
            end = (distance == 0) | (distance == half)
            holder = jnp.where(end, owner_core, jnp.where(offset > half, 0, 1))
            unit = jnp.where(distance == 0, 0, 2 * distance - jnp.where(owner_core == holder, 1, 0))
            away = jnp.where(holder == core, 0, 1)
            slot = unit + away * chips
            unit_of[r] = slot
            filled[slot] = filled[slot] + 1
            table[SECTOR, r] = local_map[t, c]
            table[LATER, r] = jnp.where((away == 1) & (unit >= early), 1, 0)

    for o in range(terms):
        table[CLASS, o] = op_class[o]

    def place_unit(u, at):
        table[START, u] = at
        count = filled[u]
        filled[u] = at
        return at + count

    table[START, 2 * chips] = lax.fori_loop(0, 2 * chips, place_unit, jnp.int32(0))

    @pl.loop(0, targets * classes)
    def _(r):
        u = unit_of[r]
        at = filled[u]
        table[ORDER, at] = r
        filled[u] = at + 1

    out = pltpu.make_async_copy(table, table_out, sems.at[1])
    out.start()
    out.wait()
    wave_copy.wait()


def fetch(near, unit, sector, target, r, sem):
    op_size = len(unit)
    me = lax.axis_index("op")
    for j, source in enumerate(unit):
        turn = lax.rem(me + j, op_size)
        if near:
            target[r, turn] = source[sector]
        else:
            pltpu.make_async_copy(source.at[sector], target.at[r, turn], sem).start()


def read_table(source, target, sem):
    copy = pltpu.make_async_copy(source, target, sem)
    copy.start()
    copy.wait()


def grouped(refs, size):
    return [refs[i : i + size] for i in range(0, len(refs), size)]


def sent_kernel(sizes, low, high, asked_in, *refs):
    op_size, chips, near = sizes[3:]
    *units, sent, table, slot_sems, sem = refs
    read_table(asked_in, table, sem)
    skipped = table[START, chips + low]
    for u, unit in enumerate(grouped(units, op_size), low):

        @pl.loop(table[START, chips + u], table[START, chips + u + 1])
        def _(i):
            slot = i - skipped
            fetch(near, unit, table[SECTOR, table[ORDER, i]], sent, slot, slot_sems.at[slot])

    if near:
        return

    @pl.loop(0, table[START, chips + high] - skipped)
    def _(slot):
        pltpu.make_async_copy(sent.at[slot], sent.at[slot], slot_sems.at[slot]).wait()


def fetch_own(near, units, low, table, blocks, block_sems):
    for u, unit in enumerate(units, low):

        @pl.loop(table[START, u], table[START, u + 1])
        def _(i):
            r = table[ORDER, i]
            fetch(near, unit, table[SECTOR, r], blocks, r, block_sems.at[r])


def fetch_received(near, received, first, last, table, blocks, block_sems):
    skipped = table[START, first]

    @pl.loop(skipped, table[START, last])
    def _(i):
        r = table[ORDER, i]
        if near:
            blocks[r] = received[i - skipped]
        else:
            pltpu.make_async_copy(received.at[i - skipped], blocks.at[r], block_sems.at[r]).start()


def wait_blocks(near, first, last, table, blocks, block_sems):
    if near:
        return

    @pl.loop(table[START, first], table[START, last])
    def _(i):
        r = table[ORDER, i]
        pltpu.make_async_copy(blocks.at[r], blocks.at[r], block_sems.at[r]).wait()


def load_kernel(sizes, early, table_in, left, right, *refs):
    *units, lefts, rights, blocks, table, block_sems, sems = refs
    loads = [
        pltpu.make_async_copy(left, lefts, sems.at[0]),
        pltpu.make_async_copy(right, rights, sems.at[1]),
    ]
    for load in loads:
        load.start()
    read_table(table_in, table, sems.at[2])
    fetch_own(sizes[5], grouped(units, sizes[3]), 0, table, blocks, block_sems)
    wait_blocks(sizes[5], 0, early, table, blocks, block_sems)
    for load in loads:
        load.wait()


def fill_kernel(sizes, early, table_in, received, *refs):
    chips = sizes[4]
    *units, _, blocks, table, block_sems, sem = refs
    read_table(table_in, table, sem)
    fetch_received(sizes[5], received, chips, chips + early, table, blocks, block_sems)
    fetch_own(sizes[5], grouped(units, sizes[3]), early, table, blocks, block_sems)
    wait_blocks(sizes[5], early, chips + early, table, blocks, block_sems)


def product_kernel(sizes, early, first, count, table_in, received, lefts, rights, _, *refs):
    targets, terms, classes, op_size, chips, near = sizes
    keep, send, blocks, table, block_sems, sem = refs
    size = lefts.shape[-1]
    rows = size // op_size
    me = lax.axis_index("op")
    read_table(table_in, table, sem)
    if first == 0:
        fetch_received(near, received, chips + early, 2 * chips, table, blocks, block_sems)
        if count < targets:
            wait_blocks(near, chips + early, 2 * chips, table, blocks, block_sems)

    @pl.loop(0, count)
    def _(step):
        t = first + step

        if count == targets and not near:

            @pl.loop(0, classes)
            def _(c):
                r = t * classes + c

                @pl.when(table[LATER, r] == 1)
                def _():
                    pltpu.make_async_copy(blocks.at[r], blocks.at[r], block_sems.at[r]).wait()

        lifted = []
        for o in range(terms):
            block = blocks[t * classes + table[CLASS, o]].reshape(size, size)
            lifted.append(
                jnp.dot(lefts[t, o], block, preferred_element_type=jnp.float32).astype(jnp.bfloat16)
            )
        total = lax.dot_general(
            jnp.concatenate(lifted, axis=1),
            jnp.concatenate([rights[t, o] for o in range(terms)], axis=1),
            (((1,), (1,)), ((), ())),
            preferred_element_type=jnp.float32,
        )
        for j in range(op_size):
            part = total[j * rows : (j + 1) * rows]
            distance = lax.rem(j + op_size - me, op_size)

            @pl.when(distance == 0)
            def _():
                keep[step] = part

            @pl.when(distance != 0)
            def _():
                send[distance - 1, step] = part.astype(jnp.bfloat16)


def held_kernel(source, out):
    del source, out


def shards(wave, left_ops, right_ops, owner_map, local_map, op_class):
    chips, op_size = lax.axis_size("chip"), lax.axis_size("op")
    targets, terms, size, _ = left_ops.shape
    sec_dev, rows, _ = wave.shape
    classes = owner_map.shape[1]
    half = chips // 2
    asked = targets * classes
    near = chips * op_size * wave.size <= 4 * 1024 * 1024
    sizes = (targets, terms, classes, op_size, chips, near)
    early = chips - 3
    most = max(2, (asked + 2 * chips - 1) // (2 * chips) + 1)
    ring = list(range(0, chips, 2)) + list(range(1, chips, 2))[::-1]

    def hop(x):
        pairs = [
            (2 * ring[i] + core, 2 * ring[(i + 1 - 2 * core) % chips] + core)
            for i in range(chips)
            for core in range(2)
        ]
        return lax.ppermute(x, ("chip", "core"), pairs)

    def swap(x):
        return lax.ppermute(x, "core", [(0, 1), (1, 0)])

    def across(x):
        return [
            lax.ppermute(x, "op", [((q + j) % op_size, q) for q in range(op_size)])
            for j in range(1, op_size)
        ]

    whole = pl.BlockSpec(memory_space=pltpu.VMEM)
    scalars = pl.BlockSpec(memory_space=pltpu.SMEM)
    apart = pl.BlockSpec(memory_space=pl.ANY)
    held_in = whole if near else apart
    def call(kernel, name, operands, outs, scratch, specs=None, aliases={}, flops=0):
        return pl.pallas_call(
            kernel,
            name=name,
            in_specs=specs or [whole] + [held_in] * (len(operands) - 1),
            out_specs=[whole] * len(outs),
            out_shape=outs,
            input_output_aliases=aliases,
            scratch_shapes=[pltpu.SMEM(TABLE, jnp.int32)] + scratch,
            compiler_params=pltpu.CompilerParams(vmem_limit_bytes=LIMITS[name] * 1024 * 1024),
            cost_estimate=pl.CostEstimate(
                flops=flops, bytes_accessed=sum(2 * x.size for x in outs), transcendentals=0
            ),
        )(*operands)

    table, wave_near = call(
        functools.partial(table_kernel, sizes, early),
        "table",
        [owner_map, local_map, op_class, wave],
        [jax.ShapeDtypeStruct(TABLE, jnp.int32), jax.ShapeDtypeStruct(wave.shape, wave.dtype)],
        [
            pltpu.SMEM((asked,), jnp.int32),
            pltpu.SMEM((2 * chips,), jnp.int32),
            pltpu.SemaphoreType.DMA((2,)),
        ],
        [scalars] * 3 + [apart],
    )

    rules = {'other': [('crossed', -2)], ('other', 2): [('own', -1)]}

    @functools.cache
    def arrived(kind, k):
        if k == 0:
            return dict(own=lambda: [wave], other=lambda: [swap(wave)], beside=lambda: across(wave))[kind]()
        x = arrived("other", k) if kind == "crossed" else arrived(kind, k - 1)
        done = []
        for before, shift in (*rules.get(kind, ()), *rules.get((kind, k), ())):
            most_hops = half - 1 if before in ("other", "crossed") else half
            if 1 <= k + shift <= most_hops:
                done += arrived(before, k + shift)
        if done:
            x = [lax.optimization_barrier((y, *done))[0] for y in x]
        if (kind, k) == ('beside', 1):
            x = [lax.optimization_barrier((y, table))[0] for y in x]
        if kind == "crossed":
            return across(x[0])
        return [hop(y) for y in x]

    units = [[wave_near] + arrived("beside", 0)]
    for k in range(1, half):
        units += [arrived("own", k) + arrived("beside", k), arrived("other", k) + arrived("crossed", k)]
    units.append(arrived("own", half) + arrived("beside", half))

    block_shape = (op_size, rows, size)
    blocks_out = jax.ShapeDtypeStruct((asked,) + block_shape, jnp.bfloat16)
    block_sems = [pltpu.SemaphoreType.DMA((asked,)), pltpu.SemaphoreType.DMA]

    def flat(low, high, ties=()):
        arrays = [x for unit in units[low:high] for x in unit]
        tied = [x for kind, k in ties for x in arrived(kind, k)]
        return arrays[:-1] + [lax.optimization_barrier((arrays[-1], *tied))[0]] if tied else arrays

    their_table = swap(table)

    def gather(low, high, arrays):
        slots = min(asked, (high - low) * most)
        (sent,) = call(
            functools.partial(sent_kernel, sizes, low, high),
            "sent",
            [their_table] + arrays,
            [jax.ShapeDtypeStruct((slots,) + block_shape, jnp.bfloat16)],
            [pltpu.SemaphoreType.DMA((slots,)), pltpu.SemaphoreType.DMA],
        )
        return swap(sent)

    first_received = gather(0, early, flat(0, early, ()))
    operators_out = [jax.ShapeDtypeStruct(x.shape, jnp.bfloat16) for x in (left_ops, right_ops)]
    lefts, rights, blocks = call(
        functools.partial(load_kernel, sizes, early),
        "load",
        [table, left_ops, right_ops] + flat(0, early, (('own', 3),)),
        operators_out + [blocks_out],
        [pltpu.SemaphoreType.DMA((asked,)), pltpu.SemaphoreType.DMA((3,))],
        [whole] + [apart] * 2 + [held_in] * (early * op_size),
    )
    late = flat(early, chips)
    received = gather(early, chips, [lax.optimization_barrier((late[0], lefts))[0]] + late[1:])
    operands = [table, first_received] + late + [blocks]
    (blocks,) = call(
        functools.partial(fill_kernel, sizes, early),
        "fill",
        operands,
        [blocks_out],
        block_sems,
        [whole] + [held_in] * (len(late) + 1) + [whole],
        {len(operands) - 1: 0},
    )

    results, held = [], []
    parts = [targets - 2, 2]
    for first, count in zip([sum(parts[:i]) for i in range(len(parts))], parts):
        keep, send, blocks = call(
            functools.partial(product_kernel, sizes, early, first, count),
            "product",
            [table, received, lefts, rights, blocks],
            [
                jax.ShapeDtypeStruct((count, rows, size), jnp.float32),
                jax.ShapeDtypeStruct((op_size - 1, count, rows, size), jnp.bfloat16),
                blocks_out,
            ],
            block_sems,
            [whole, held_in] + [whole] * 3,
            {4: 2},
            4 * count * terms * size**3,
        )
        for k in range(1, op_size):
            turn = [(p, (p + k) % op_size) for p in range(op_size)]
            part = lax.ppermute(send[k - 1], "op", turn)
            if first + count < targets:
                part = pl.pallas_call(
                    held_kernel,
                    name="held",
                    in_specs=[apart],
                    out_specs=apart,
                    out_shape=jax.ShapeDtypeStruct(part.shape, part.dtype),
                    input_output_aliases={0: 0},
                    cost_estimate=pl.CostEstimate(
                        flops=0, bytes_accessed=100 * part.size, transcendentals=0
                    ),
                )(part)
                held.append(part)
            elif held:
                keep = lax.optimization_barrier((keep, *held))[0]
            keep = keep + part.astype(jnp.float32)
        results.append(keep.astype(jnp.bfloat16))
    return jnp.concatenate(results)


def solution(mesh):
    sec_size, op_size = mesh.shape["sec"], mesh.shape["op"]
    split = Mesh(mesh.devices.reshape(sec_size // 2, 2, op_size), ("chip", "core", "op"))
    sec = ("chip", "core")
    in_specs = (
        P(sec, "op", None),
        P(sec, "op", None, None),
        P(sec, "op", None, None),
        P(sec, None),
        P(sec, None),
        P("op"),
    )
    out_specs = P(sec, "op", None)
    return jax.shard_map(shards, mesh=split, in_specs=in_specs, out_specs=out_specs, check_vma=False)
```
